128 devices in a mesh: section: 4 (over z), dev: 32 (over y, x, core).
Axes of the slice: x: 4, y: 4, z: 4, core: 2. Of those that a mesh axis runs over, the one named last changes fastest.
Arguments:
- points: float32 [3, 3, 524288], P(None, None, ('section', 'dev')), may hold values from -1 to 1
- weights: float32 [3, 524288], P(None, ('section', 'dev')), may hold values from 0.2 to 0.5
- density: float32 [2, 524288], P(None, ('section', 'dev')), may hold values from -6 to 6
- near_pairs: int32 [3, 16384], P(None, ('section', 'dev')), may hold values from 0 to 4095, as said below
- gap_pairs: int32 [3, 4096], P(None, ('section', 'dev')), may hold values from 0 to 4095, as said below
Outputs:
- potentials: float32 [2, 524288], P(None, ('section', 'dev'))
The draws below stay inside these ranges and needn't reach their ends.
Inputs may be any that keep to these rules, and one draw needn't show every extreme that they name: `near_pairs`: column t belongs to device t // 128 of section+dev. Row 0 names a cluster held by that device, row 1 a cluster held by a device of the same section whose dev index differs from the owner's by at most 2, row 2 is 0 or 1. The first 32 columns of each device are the self pairs of its clusters in order and are always listed; column 32 of each device is listed and names a cluster exactly 2 dev indices away; some device lists all its columns. `gap_pairs`: column t belongs to device t // 32 of section+dev. Row 0 names a cluster held by that device, row 1 a cluster of another section held by the device of the same index along dev, row 2 is 0 or 1; some device lists all its columns.
All inputs are finite; a program needn't handle non-finite values.
Results may differ from the reference program's by a relative error of at most 0.0001.
Values sent between devices are 32-bit elements; how exact they have to be, the bound alone decides.
No kernel may reach another device: no remote copies, remote signals or barrier semaphores. Data moves between devices by JAX's collectives and lax.ppermute only.
A program may use at most 64 MiB of HBM per device.

```python
import math
import jax
import jax.numpy as jnp
from jax import lax

PANEL_CL = 128
QUAD = 3
CL_DEV = 32
NEAR_DEV = 128
GAP_DEV = 32
SEC_CL = 1024
CLUSTERS = 4096
PANELS = 524288
NEAR_TOTAL = 16384
GAP_TOTAL = 4096


def live_counts(key, owners, most):
    key_a, key_b = jax.random.split(key)
    counts = jax.random.randint(key_a, (owners,), most // 3, most + 1, dtype=jnp.int32)
    fullest = jax.random.randint(key_b, (), 0, owners, dtype=jnp.int32)
    return jnp.where(jnp.arange(owners, dtype=jnp.int32) == fullest, most, counts)


def slot_ranks(key, owners, per_owner):
    keys = jax.random.split(key, owners)

    def rank_row(row_key):
        return jax.random.permutation(row_key, per_owner).astype(jnp.int32)
    return jax.vmap(rank_row)(keys)


def draw_near_pairs(key, part):
    owners = NEAR_TOTAL // NEAR_DEV
    extras = NEAR_DEV - CL_DEV
    dev_count = SEC_CL // CL_DEV
    key_a, key_b, key_c, key_d, key_e = jax.random.split(jax.random.fold_in(key, 11), 5)
    owner = jnp.arange(owners, dtype=jnp.int32)[:, None]
    within = jnp.arange(NEAR_DEV, dtype=jnp.int32)[None, :]
    section = owner * CL_DEV // SEC_CL
    dev_place = owner % dev_count
    local_pick = jax.random.randint(key_a, (owners, NEAR_DEV), 0, CL_DEV, dtype=jnp.int32)
    first = owner * CL_DEV + jnp.where(within < CL_DEV, within, local_pick)
    offset = jax.random.randint(key_b, (owners, NEAR_DEV), -2, 3, dtype=jnp.int32)
    forced = jnp.where(dev_place <= dev_count - 3, 2, -2).astype(jnp.int32)
    offset = jnp.where(within == CL_DEV, forced, offset)
    target = dev_place + offset
    target = jnp.where((target < 0) | (target >= dev_count), dev_place - offset, target)
    partner = section * SEC_CL + target * CL_DEV + jax.random.randint(key_e, (owners, NEAR_DEV), 0, CL_DEV, dtype=jnp.int32)
    second = jnp.where(within < CL_DEV, first, partner)
    counts = live_counts(key_c, owners, extras)
    ranks = slot_ranks(key_d, owners, extras)
    live_extra = (ranks < counts[:, None]).astype(jnp.int32)
    live_extra = jnp.where(jnp.arange(extras, dtype=jnp.int32)[None, :] == 0, 1, live_extra).astype(jnp.int32)
    live = jnp.concatenate([jnp.ones((owners, CL_DEV), jnp.int32), live_extra], 1)
    return jnp.stack([first.reshape(-1), second.reshape(-1), live.reshape(-1)], 0)


def draw_gap_pairs(key, part):
    owners = GAP_TOTAL // GAP_DEV
    sections = CLUSTERS // SEC_CL
    key_a, key_b, key_c, key_d, key_e = jax.random.split(jax.random.fold_in(key, 23), 5)
    owner = jnp.arange(owners, dtype=jnp.int32)[:, None]
    section = owner * CL_DEV // SEC_CL
    dev_place = owner % (SEC_CL // CL_DEV)
    first = owner * CL_DEV + jax.random.randint(key_a, (owners, GAP_DEV), 0, CL_DEV, dtype=jnp.int32)
    other = (section + jax.random.randint(key_b, (owners, GAP_DEV), 1, sections, dtype=jnp.int32)) % sections
    second = other * SEC_CL + dev_place * CL_DEV + jax.random.randint(key_c, (owners, GAP_DEV), 0, CL_DEV, dtype=jnp.int32)
    counts = live_counts(key_d, owners, GAP_DEV)
    ranks = slot_ranks(key_e, owners, GAP_DEV)
    live = (ranks < counts[:, None]).astype(jnp.int32)
    return jnp.stack([first.reshape(-1), second.reshape(-1), live.reshape(-1)], 0)


def level_of(own_key, extent, pieces, smallest, top_value):
    factor_of, own = 1.0, jax.random.fold_in(own_key, 6)
    for position, shards_of in pieces:
        heights = jnp.exp(jax.random.uniform(jax.random.fold_in(own, position), (shards_of,), jnp.float32, smallest / len(pieces), top_value / len(pieces)))
        factor_of = factor_of * jnp.repeat(heights, extent[position] // shards_of).reshape([-1 if axis == position else 1 for axis in range(len(extent))])
    return factor_of


def bell_draw(own_key, dims, scale, bound, cuts=(), held_as=jnp.bfloat16):
    values = jax.random.normal(own_key, dims, jnp.float32) * scale
    if len(cuts) > 0:
        values = level_of(own_key, dims, cuts, -0.22, 0.18) * values
    return jnp.clip(values, min=-bound, max=bound).astype(held_as)


def setup_inputs(seed: int = 0) -> dict:
    key_of = jax.random.split(jax.random.key(seed), 6)
    return {
        "points": jnp.clip(jax.random.uniform(key_of[0], (3, QUAD, PANELS), jnp.float32, -1.0, 1.0) * level_of(key_of[0], (3, QUAD, PANELS), ((2, 128),), -0.4, 0.0), -1.0, 1.0),
        "weights": jnp.clip(jnp.exp(math.log(0.5) - 0.9162907 * jax.random.uniform(key_of[1], (QUAD, PANELS), jnp.float32) ** level_of(key_of[1], (QUAD, PANELS), ((1, 128),), -0.2, 0.2)), 0.2, 0.5),
        "density": bell_draw(key_of[2], (2, PANELS), 1.0, 6.0, ((1, 128),), jnp.float32),
        "near_pairs": draw_near_pairs(jax.random.fold_in(key_of[5], 71), 0),
        "gap_pairs": draw_gap_pairs(jax.random.fold_in(key_of[5], 71), 0),
    }


smoothing = 0.02
green_scale = 0.25 / math.pi

def pair_terms(block_a, block_b, listed, twice):
    groups, rows_count, width = block_a.shape
    quad_count = (rows_count - 2) // 4
    pos_a = block_a[:, :3 * quad_count].reshape(groups, 3, quad_count, width)
    pos_b = block_b[:, :3 * quad_count].reshape(groups, 3, quad_count, width)
    w_a = block_a[:, 3 * quad_count:4 * quad_count]
    w_b = block_b[:, 3 * quad_count:4 * quad_count]
    dens_a = block_a[:, 4 * quad_count:]
    dens_b = block_b[:, 4 * quad_count:]
    term_a = jnp.zeros((groups, 2, width), jnp.float32)
    term_b = jnp.zeros((groups, 2, width), jnp.float32)
    for point_a in range(quad_count):
        load_a = w_a[:, point_a, None, :] * dens_a
        for point_b in range(quad_count):
            load_b = w_b[:, point_b, None, :] * dens_b
            step_x = pos_a[:, 0, point_a, :, None] - pos_b[:, 0, point_b, None, :]
            step_y = pos_a[:, 1, point_a, :, None] - pos_b[:, 1, point_b, None, :]
            step_z = pos_a[:, 2, point_a, :, None] - pos_b[:, 2, point_b, None, :]
            distance = step_x * step_x + step_y * step_y + step_z * step_z + smoothing * smoothing
            kernel_tile = green_scale / jnp.sqrt(distance)
            term_a = term_a + w_a[:, point_a, None, :] * jnp.einsum('gab,grb->gra', kernel_tile, load_b, precision=lax.Precision.HIGHEST)
            term_b = term_b + w_b[:, point_b, None, :] * jnp.einsum('gab,gra->grb', kernel_tile, load_a, precision=lax.Precision.HIGHEST)
    term_a = term_a * listed[:, None, None]
    term_b = term_b * (listed * twice)[:, None, None]
    return (term_a, term_b)

def reference(points, weights, density, near_pairs, gap_pairs):
    panel_table = jnp.concatenate([points.reshape(3 * QUAD, PANELS), weights, density], 0)
    rows_count = panel_table.shape[0]
    blocks = panel_table.reshape(rows_count, CLUSTERS, PANEL_CL)
    firsts = jnp.concatenate([near_pairs[0], gap_pairs[0]]).astype(jnp.int32)
    seconds = jnp.concatenate([near_pairs[1], gap_pairs[1]]).astype(jnp.int32)
    listed = jnp.concatenate([near_pairs[2], gap_pairs[2]]).astype(jnp.float32)
    twice = (firsts != seconds).astype(jnp.float32)
    group_size = 8
    step_count = firsts.shape[0] // group_size

    def one_step(totals, items):
        first_set, second_set, live_set, twice_set = items
        block_a = jnp.transpose(blocks[:, first_set], (1, 0, 2))
        block_b = jnp.transpose(blocks[:, second_set], (1, 0, 2))
        term_a, term_b = pair_terms(block_a, block_b, live_set, twice_set)
        totals = totals.at[:, first_set].add(jnp.transpose(term_a, (1, 0, 2)))
        totals = totals.at[:, second_set].add(jnp.transpose(term_b, (1, 0, 2)))
        return (totals, None)
    items = (firsts.reshape(step_count, group_size), seconds.reshape(step_count, group_size), listed.reshape(step_count, group_size), twice.reshape(step_count, group_size))
    totals, unused = lax.scan(one_step, jnp.zeros((2, CLUSTERS, PANEL_CL), jnp.float32), items)
    return totals.reshape(2, PANELS)
```

```python
import functools
import math

import jax
import jax.numpy as jnp
from jax import lax
from jax.experimental import pallas as pl
from jax.experimental.pallas import tpu as pltpu
from jax.sharding import PartitionSpec as P

CL = 128
QUAD = 3
DEPTH = 48
UNROLL = 4

smoothing = 0.02
green_scale = 0.25 / math.pi
f32 = jnp.float32
bf16 = jnp.bfloat16


def rounded(x, magic):
    return (x + magic) - magic


def row_ids():
    return lax.broadcasted_iota(jnp.int32, (8, CL), 0)


def parts_of(tile, row_limit):
    rows = row_ids()
    live = jnp.logical_and(lax.rem(rows, 4) < 3, rows < row_limit)
    x = jnp.where(live, tile, 0.0)
    high = rounded(x, 49152.0)
    rest = x - high
    mid = rounded(rest, 96.0)
    low = rounded(rest - mid, 0.1875)
    rest = mid + low
    sq_high = high * high
    sq_rest = rest * (high + high + rest)

    def row_sum(v):
        u = v + pltpu.roll(v, 7, 0)
        return u + pltpu.roll(u, 6, 0)

    return high, mid, low, row_sum(sq_high), row_sum(sq_rest)


def square_parts(sum_high, sum_rest):
    rows = row_ids()
    upper = rows < 4
    v = jnp.where(upper, sum_high, sum_rest)
    one = rounded(v, jnp.where(upper, 196608.0, 768.0))
    rest = v - one
    two = rounded(rest, jnp.where(upper, 768.0, 3.0))
    three = rest - two
    place = lax.rem(rows, 4)
    return jnp.where(place == 0, one, jnp.where(place == 1, two, jnp.where(place == 2, three, 0.0)))


def point_features(tile0, tile1):
    h0, m0, l0, sh0, sr0 = parts_of(tile0, 8)
    h1, m1, l1, sh1, sr1 = parts_of(tile1, 3)

    def spread(v, row):
        return jnp.broadcast_to(v[row : row + 1], (8, CL))

    turn = lambda v: pltpu.roll(v, 4, 0)
    return (
        (h0, m0, l0, turn(l0), spread(sh0, 0), spread(sr0, 0)),
        (turn(h0), turn(m0), turn(l0), l0, spread(sh0, 4), spread(sr0, 4)),
        (h1, m1, l1, turn(l1), spread(sh1, 0), spread(sr1, 0)),
    )


def right_features(tile0, tile1):
    rows = row_ids()
    out = []
    for high, mid, low, low_turned, sum_high, sum_rest in point_features(tile0, tile1):
        ones = jnp.where(rows < 6, 1.0, 0.0)
        g0 = jnp.where(rows < 3, high, ones)
        g1 = square_parts(sum_high, sum_rest + smoothing * smoothing)
        g4 = jnp.where(rows < 4, mid, low_turned)
        out.append(jnp.concatenate([g0, g1, g0, g0, g4, g4], 0).astype(bf16))
    return out


def left_features(tile0, tile1):
    rows = row_ids()
    out = []
    for high, mid, low, low_turned, sum_high, sum_rest in point_features(tile0, tile1):
        sq = square_parts(sum_high, sum_rest)
        sq_high = pltpu.roll(sq, 3, 0)
        sq_rest = pltpu.roll(sq, 7, 0)
        first = rows < 3
        mids = jnp.logical_and(rows >= 3, rows < 6)
        h2 = jnp.where(first, -2.0 * high, 0.0)
        m2 = jnp.where(first, -2.0 * mid, 0.0)
        l2 = jnp.where(first, -2.0 * low, 0.0)
        b0 = jnp.where(mids, sq_high, h2)
        b1 = jnp.where(lax.rem(rows, 4) < 3, 1.0, 0.0)
        b2 = jnp.where(mids, sq_rest, m2)
        b4 = h2 + pltpu.roll(h2, 4, 0)
        b5 = m2 + pltpu.roll(m2, 4, 0)
        out.append(jnp.concatenate([b0, b1, b2, l2, b4, b5], 0))
    return out


def pair_kernel(kind, tables, clusters, *refs):
    pairs, local = refs[0], refs[1]
    others = refs[2 : 2 + tables] if kind != "local" else (local,)
    refs = refs[2 + (tables if kind != "local" else 0) :]
    out_a, out_b = refs[0], refs[1]
    todo, left, right, raw, wide_w, wide_d, acc_a, acc_b = refs[2:]
    slots = pairs.shape[1]
    cl_bits = clusters.bit_length() - 1

    def collect(t, count):
        first, second, listed = pairs[0, t], pairs[1, t], pairs[2, t]
        i = jnp.bitwise_and(first, clusters - 1)
        j = jnp.bitwise_and(second, clusters - 1)
        if kind == "gap":
            sec_bits = cl_bits + 5
            step = jnp.bitwise_and(
                lax.shift_right_logical(second, sec_bits) - lax.shift_right_logical(first, sec_bits) + 4, 3
            )
            table = step - 1
            take = listed
        else:
            step = lax.shift_right_logical(second, cl_bits) - lax.shift_right_logical(first, cl_bits)
            here = (step == 0).astype(jnp.int32)
            if kind == "local":
                table = 0
                take = listed * here
            else:
                table = jnp.where(step < 0, step + 2, step + 1)
                take = listed * (1 - here)
        twice = (first != second).astype(jnp.int32)
        todo[0, count] = i
        todo[1, count] = table * clusters + j
        todo[2, count] = 1
        todo[3, count] = twice
        return count + take

    count = lax.fori_loop(0, slots, collect, 0)
    for extra in range(UNROLL - 1):
        todo[0, count + extra] = 0
        todo[1, count + extra] = 0
        todo[2, count + extra] = 0
        todo[3, count + extra] = 0

    def prepare_left(c, carry):
        lanes = pl.ds(pl.multiple_of(c * CL, CL), CL)
        tile0, tile1 = local[0:8, lanes], local[8:16, lanes]
        weight_rows = (tile0[3:4], tile0[7:8], tile1[3:4])
        dens_rows = (tile1[4:5], tile1[5:6])
        for q, block in enumerate(left_features(tile0, tile1)):
            block = jnp.concatenate([block, jnp.zeros((CL - DEPTH, CL), f32)], 0)
            left[c, q * CL : (q + 1) * CL, :] = jnp.transpose(block).astype(bf16)
            wide_w[c, q * CL : (q + 1) * CL, :] = jnp.transpose(
                jnp.broadcast_to(weight_rows[q] * green_scale, (CL, CL))
            )
        for r in range(2):
            wide_d[c, r * CL : (r + 1) * CL, :] = jnp.transpose(jnp.broadcast_to(dens_rows[r], (CL, CL)))
        acc_a[c] = jnp.zeros((2 * CL, CL), f32)
        return carry

    lax.fori_loop(0, clusters, prepare_left, 0)

    def prepare_right(table, ref):
        def body(c, carry):
            lanes = pl.ds(pl.multiple_of(c * CL, CL), CL)
            tile0, tile1 = ref[0:8, lanes], ref[8:16, lanes]
            place = table * clusters + c
            for q, block in enumerate(right_features(tile0, tile1)):
                right[place, :, q * CL : (q + 1) * CL] = block
            raw[place, 0:8, :] = tile0
            raw[place, 8:16, :] = tile1
            acc_b[place] = jnp.zeros((16, CL), f32)
            return carry

        lax.fori_loop(0, clusters, body, 0)

    for table in range(len(others)):
        prepare_right(table, others[table])

    def tile_of(i, j):
        weight_b = (raw[j, 3:4, :], raw[j, 7:8, :], raw[j, 11:12, :])
        far = right[j]
        total = None
        for p in range(QUAD):
            near = left[i, p * CL : (p + 1) * CL, 0:DEPTH]
            dist = jnp.dot(near, far, preferred_element_type=f32)
            row = None
            for q in range(QUAD):
                term = weight_b[q] * lax.rsqrt(dist[:, q * CL : (q + 1) * CL])
                row = term if row is None else row + term
            row = row * wide_w[i, p * CL : (p + 1) * CL, :]
            total = row if total is None else total + row
        return total

    def group(g, carry):
        done = []
        for u in range(UNROLL):
            t = g * UNROLL + u
            i, j = todo[0, t], todo[1, t]
            listed, twice = todo[2, t].astype(f32), todo[3, t].astype(f32)
            tile = tile_of(i, j)
            terms_b = []
            for r in range(2):
                product = tile * wide_d[i, r * CL : (r + 1) * CL, :]
                part = product[0:8]
                for k in range(1, CL // 8):
                    part = part + product[8 * k : 8 * k + 8]
                terms_b.append(part * twice)
            done.append((i, j, listed, tile, terms_b))
        for i, j, listed, tile, terms_b in done:
            for r in range(2):
                acc_b[j, 8 * r : 8 * r + 8, :] += terms_b[r]
                acc_a[i, r * CL : (r + 1) * CL, :] += tile * (raw[j, 12 + r : 13 + r, :] * listed)
        return carry

    lax.fori_loop(0, lax.div(count + UNROLL - 1, UNROLL), group, 0)

    def finish_a(c, carry):
        lanes = pl.ds(pl.multiple_of(c * CL, CL), CL)
        value = acc_a[c]
        high = value.astype(bf16)
        low = (value - high.astype(f32)).astype(bf16)
        both = jnp.concatenate([high, low], 1)
        ones = jnp.ones((8, 2 * CL), bf16)
        sums = lax.dot_general(ones, both, (((1,), (1,)), ((), ())), preferred_element_type=f32)
        rows = [sums[0:1, 0:CL], sums[0:1, CL : 2 * CL]]
        if kind == "local":
            for r in range(2):
                rows[r] = rows[r] + jnp.sum(acc_b[c, 8 * r : 8 * r + 8, :], 0, keepdims=True)
        for r in range(2):
            out_a[r : r + 1, lanes] = rows[r]
        return carry

    lax.fori_loop(0, clusters, finish_a, 0)

    for table in range(len(others)):
        if kind == "local":
            continue

        def finish_b(c, carry):
            lanes = pl.ds(pl.multiple_of(c * CL, CL), CL)
            for r in range(2):
                out_b[table, r : r + 1, lanes] = jnp.sum(
                    acc_b[table * clusters + c, 8 * r : 8 * r + 8, :], 0, keepdims=True
                )
            return carry

        lax.fori_loop(0, clusters, finish_b, 0)
    if kind == "local":
        out_b[...] = jnp.zeros_like(out_b)


def pair_sums(kind, pairs, local, others):
    panels = local.shape[1]
    clusters = panels // CL
    tables = max(len(others), 1)
    places = tables * clusters
    whole = pl.BlockSpec(memory_space=pltpu.VMEM)
    out_b_shape = (1, 8, CL) if kind == "local" else (tables, 2, panels)
    return pl.pallas_call(
        functools.partial(pair_kernel, kind, tables, clusters),
        out_shape=[
            jax.ShapeDtypeStruct((2, panels), f32),
            jax.ShapeDtypeStruct(out_b_shape, f32),
        ],
        in_specs=[pl.BlockSpec(memory_space=pltpu.SMEM)] + [whole] * (1 + len(others)),
        out_specs=[whole, whole],
        scratch_shapes=[
            pltpu.SMEM((4, pairs.shape[1] + UNROLL), jnp.int32),
            pltpu.VMEM((clusters, QUAD * CL, CL), bf16),
            pltpu.VMEM((places, DEPTH, QUAD * CL), bf16),
            pltpu.VMEM((places, 16, CL), f32),
            pltpu.VMEM((clusters, QUAD * CL, CL), f32),
            pltpu.VMEM((clusters, 2 * CL, CL), f32),
            pltpu.VMEM((clusters, 2 * CL, CL), f32),
            pltpu.VMEM((places, 16, CL), f32),
        ],
        compiler_params=pltpu.CompilerParams(vmem_limit_bytes=56 * 1024 * 1024),
        name="pairs_" + kind,
    )(pairs, local, *others)


def pack_kernel(points, weights, density, out):
    for q in range(QUAD):
        for c in range(3):
            out[4 * q + c : 4 * q + c + 1, :] = points[c, q : q + 1, :]
        out[4 * q + 3 : 4 * q + 4, :] = weights[q : q + 1, :]
    out[12:14, :] = density[...]
    out[14:16, :] = jnp.zeros((2, out.shape[1]), f32)


def packed(points, weights, density):
    whole = pl.BlockSpec(memory_space=pltpu.VMEM)
    return pl.pallas_call(
        pack_kernel,
        out_shape=jax.ShapeDtypeStruct((16, points.shape[2]), f32),
        in_specs=[whole] * 3,
        out_specs=whole,
        name="pack",
    )(points, weights, density)


def from_offset(block, axis, offset, ring):
    size = lax.axis_size(axis)
    if ring:
        route = [((i + offset) % size, i) for i in range(size)]
    else:
        route = [(i + offset, i) for i in range(size) if 0 <= i + offset < size]
    return lax.ppermute(block, axis, route)


near_offsets = (-2, -1, 1, 2)
gap_offsets = (1, 2, 3)


def per_device(points, weights, density, near_pairs, gap_pairs):
    local = packed(points, weights, density)
    near_tables = [from_offset(local, "dev", o, False) for o in near_offsets]
    gap_tables = [from_offset(local, "section", o, True) for o in gap_offsets]
    total, _ = pair_sums("local", near_pairs, local, [])
    near_a, near_b = pair_sums("near", near_pairs, local, near_tables)
    gap_a, gap_b = pair_sums("gap", gap_pairs, local, gap_tables)
    total = total + near_a + gap_a
    for place, offset in enumerate(near_offsets):
        total = total + from_offset(near_b[place], "dev", -offset, False)
    for place, offset in enumerate(gap_offsets):
        total = total + from_offset(gap_b[place], "section", -offset, True)
    return total


def solution(mesh):
    placed = (
        P(None, None, ("section", "dev")),
        P(None, ("section", "dev")),
        P(None, ("section", "dev")),
        P(None, ("section", "dev")),
        P(None, ("section", "dev")),
    )
    return jax.shard_map(
        per_device,
        mesh=mesh,
        in_specs=placed,
        out_specs=P(None, ("section", "dev")),
        check_vma=False,
    )
```

```python
import functools
import math

import jax
import jax.numpy as jnp
from jax import lax
from jax.experimental import pallas as pl
from jax.experimental.pallas import tpu as pltpu
from jax.sharding import PartitionSpec as P

CL = 128
QUAD = 3
DEPTH = 48
TURNED = 64
UNROLL = 4

smoothing = 0.02
green_scale = 0.25 / math.pi
f32 = jnp.float32
bf16 = jnp.bfloat16


def rounded(x, magic):
    return (x + magic) - magic


def row_ids(like):
    return lax.broadcasted_iota(jnp.int32, like.shape, 0)


def parts_of(tile, row_limit):
    rows = row_ids(tile)
    live = jnp.logical_and(lax.rem(rows, 4) < 3, rows < row_limit)
    x = jnp.where(live, tile, 0.0)
    high = rounded(x, 49152.0)
    rest = x - high
    mid = rounded(rest, 96.0)
    low = rounded(rest - mid, 0.1875)
    rest = mid + low
    sq_high = high * high
    sq_rest = rest * (high + high + rest)

    def row_sum(v):
        u = v + pltpu.roll(v, 7, 0)
        return u + pltpu.roll(u, 6, 0)

    return high, mid, low, row_sum(sq_high), row_sum(sq_rest)


def square_parts(sum_high, sum_rest):
    rows = row_ids(sum_high)
    upper = rows < 4
    v = jnp.where(upper, sum_high, sum_rest)
    one = rounded(v, jnp.where(upper, 196608.0, 768.0))
    rest = v - one
    two = rounded(rest, jnp.where(upper, 768.0, 3.0))
    three = rest - two
    place = lax.rem(rows, 4)
    return jnp.where(place == 0, one, jnp.where(place == 1, two, jnp.where(place == 2, three, 0.0)))


def point_features(tile0, tile1):
    h0, m0, l0, sh0, sr0 = parts_of(tile0, 8)
    h1, m1, l1, sh1, sr1 = parts_of(tile1, 3)

    def spread(v, row):
        return jnp.broadcast_to(v[row : row + 1], v.shape)

    turn = lambda v: pltpu.roll(v, 4, 0)
    return (
        (h0, m0, l0, turn(l0), spread(sh0, 0), spread(sr0, 0)),
        (turn(h0), turn(m0), turn(l0), l0, spread(sh0, 4), spread(sr0, 4)),
        (h1, m1, l1, turn(l1), spread(sh1, 0), spread(sr1, 0)),
    )


def right_features(tile0, tile1):
    rows = row_ids(tile0)
    out = []
    for high, mid, low, low_turned, sum_high, sum_rest in point_features(tile0, tile1):
        ones = jnp.where(rows < 6, 1.0, 0.0)
        g0 = jnp.where(rows < 3, high, jnp.where(rows < 6, ones, pltpu.roll(mid, 6, 0)))
        g1 = square_parts(sum_high, sum_rest + smoothing * smoothing)
        g1 = jnp.where(rows == 7, pltpu.roll(mid, 5, 0), g1)
        g4 = jnp.where(rows < 4, mid, low_turned)
        out.append(jnp.concatenate([g0, g1, g0, g0, g4, g4], 0).astype(bf16))
    return out


def left_features(tile0, tile1):
    rows = row_ids(tile0)
    out = []
    for high, mid, low, low_turned, sum_high, sum_rest in point_features(tile0, tile1):
        sq = square_parts(sum_high, sum_rest)
        sq_high = pltpu.roll(sq, 3, 0)
        sq_rest = pltpu.roll(sq, 7, 0)
        first = rows < 3
        mids = jnp.logical_and(rows >= 3, rows < 6)
        h2 = jnp.where(first, -2.0 * high, 0.0)
        m2 = jnp.where(first, -2.0 * mid, 0.0)
        l2 = jnp.where(first, -2.0 * low, 0.0)
        b0 = jnp.where(mids, sq_high, h2)
        b1 = jnp.where(lax.rem(rows, 4) < 3, 1.0, jnp.where(rows == 7, pltpu.roll(l2, 5, 0), 0.0))
        b3 = jnp.where(rows < 6, l2, pltpu.roll(l2, 6, 0))
        b2 = jnp.where(mids, sq_rest, m2)
        b4 = h2 + pltpu.roll(h2, 4, 0)
        b5 = m2 + pltpu.roll(m2, 4, 0)
        out.append(jnp.concatenate([b0, b1, b2, b3, b4, b5], 0))
    return out


def pair_codes(local, others, codes):
    def lists(table, row):
        return [table[row : row + 1, k * CL : (k + 1) * CL].astype(jnp.int32) for k in range(3)]

    low5 = lambda v: jnp.bitwise_and(v, 31)
    up5 = lambda v: lax.shift_right_logical(v, 5)

    def coded(valid, here, slot, there):
        return jnp.where(valid, low5(here) + (slot * 32 + low5(there)) * 256, -1)

    first, second, listed = lists(local, 14)
    me = jnp.broadcast_to(up5(first[:, 0:1]), first.shape)
    my_dev, dev = low5(me), low5(up5(second))
    slot = jnp.full(first.shape, 4, jnp.int32)
    slot = jnp.where(dev == jnp.bitwise_xor(my_dev, 2), 3, slot)
    slot = jnp.where(dev == jnp.bitwise_xor(my_dev + 1, 1) - 1, 2, slot)
    slot = jnp.where(dev == jnp.bitwise_xor(my_dev, 1), 1, slot)
    slot = jnp.where(dev == my_dev, 0, slot)
    codes[0:1, :] = coded(listed > 0, first, slot, second)
    inside = jnp.logical_and(slot == 0, first != second)
    codes[1:2, :] = coded(jnp.logical_and(listed > 0, inside), second, 0, first)
    for slot_in in range(1, 5):
        first, second, listed = lists(others[slot_in - 1], 14)
        valid = jnp.logical_and(listed > 0, up5(second) == me)
        codes[1 + slot_in : 2 + slot_in, :] = coded(valid, second, slot_in, first)
    first, second, listed = lists(local, 15)
    slot = 4 + jnp.bitwise_xor(up5(me), up5(up5(second)))
    row = coded(listed > 0, first, slot, second)
    lanes = lax.broadcasted_iota(jnp.int32, row.shape, 1)
    for slot_in in range(5, 8):
        first, second, listed = lists(others[slot_in - 1], 15)
        valid = jnp.logical_and(listed > 0, up5(second) == me)
        incoming = coded(valid, second, slot_in, first)
        row = jnp.where(lanes < 32 * (slot_in - 4), row, pltpu.roll(incoming, 32 * (slot_in - 4), 1))
    codes[6:7, :] = row
    codes[7:8, :] = jnp.full(row.shape, -1, jnp.int32)


WIDE = 4


def pair_kernel(clusters, *refs):
    tables = refs[:8]
    local = tables[0]
    out = refs[8]
    codes, codes_smem, sem, todo, left, right, raw, wide_w, acc = refs[9:]

    pair_codes(local, tables[1:], codes)
    copy = pltpu.make_async_copy(codes, codes_smem, sem)
    copy.start()

    def prepare_left(n, carry):
        for u in range(2):
            c = n * 2 + u
            lanes = pl.ds(pl.multiple_of(c * CL, CL), CL)
            tile0, tile1 = local[0:8, lanes], local[8:16, lanes]
            weight_rows = (tile0[3:4], tile0[7:8], tile1[3:4])
            for q, block in enumerate(left_features(tile0, tile1)):
                weight = jnp.broadcast_to(weight_rows[q] * green_scale, (8, CL))
                block = jnp.concatenate([block, weight, jnp.zeros((TURNED - DEPTH - 8, CL), f32)], 0)
                turned = jnp.transpose(block)
                left[c, q * CL : (q + 1) * CL, 0:TURNED] = turned.astype(bf16)
                wide_w[c, q * CL : (q + 1) * CL, :] = jnp.broadcast_to(turned[:, DEPTH : DEPTH + 1], (CL, CL))
            acc[c] = jnp.zeros((2 * CL, CL), f32)
        return carry

    lax.fori_loop(0, clusters // 2, prepare_left, 0)
    copy.wait()

    steps = clusters // WIDE
    count = 0
    for table in range(8):

        def prepare_right(n, count):
            lanes = pl.ds(pl.multiple_of(n * (WIDE * CL), WIDE * CL), WIDE * CL)
            tile0, tile1 = tables[table][0:8, lanes], tables[table][8:16, lanes]
            blocks = right_features(tile0, tile1)
            for u in range(WIDE):
                place = table * clusters + n * WIDE + u
                cut = slice(u * CL, (u + 1) * CL)
                for q in range(QUAD):
                    right[place, :, q * CL : (q + 1) * CL] = blocks[q][:, cut]
                raw[place, 0:8, :] = tile0[:, cut]
                raw[place, 8:16, :] = tile1[:, cut]
            for u in range(CL // 8):
                code = codes_smem[table, n * (CL // 8) + u]
                todo[count] = code
                count = count + (code >= 0).astype(jnp.int32)
            return count

        count = lax.fori_loop(0, steps, prepare_right, count)
    for extra in range(UNROLL - 1):
        todo[count + extra] = clusters

    def tile_of(i, j):
        weight_b = (raw[j, 3:4, :], raw[j, 7:8, :], raw[j, 11:12, :])
        far = right[j]
        total = None
        for p in range(QUAD):
            near = left[i, p * CL : (p + 1) * CL, 0:DEPTH]
            dist = jnp.dot(near, far, preferred_element_type=f32)
            row = None
            for q in range(QUAD):
                term = weight_b[q] * lax.rsqrt(dist[:, q * CL : (q + 1) * CL])
                row = term if row is None else row + term
            row = row * wide_w[i, p * CL : (p + 1) * CL, :]
            total = row if total is None else total + row
        return total

    def group(g, carry):
        done = []
        for u in range(UNROLL):
            code = todo[g * UNROLL + u]
            i = jnp.bitwise_and(code, 255)
            j = lax.shift_right_logical(code, 8)
            done.append((i, j, tile_of(i, j)))
        for i, j, tile in done:
            for r in range(2):
                acc[i, r * CL : (r + 1) * CL, :] += tile * raw[j, 12 + r : 13 + r, :]
        return carry

    lax.fori_loop(0, lax.div(count + UNROLL - 1, UNROLL), group, 0)

    def finish(n, carry):
        for u in range(4):
            c = n * 4 + u
            lanes = pl.ds(pl.multiple_of(c * CL, CL), CL)
            value = acc[c]
            high = value.astype(bf16)
            low = (value - high.astype(f32)).astype(bf16)
            both = jnp.concatenate([high, low], 1)
            ones = jnp.ones((8, 2 * CL), bf16)
            sums = lax.dot_general(ones, both, (((1,), (1,)), ((), ())), preferred_element_type=f32)
            for r in range(2):
                out[r : r + 1, lanes] = sums[0:1, r * CL : (r + 1) * CL]
        return carry

    lax.fori_loop(0, clusters // 4, finish, 0)


def pair_sums(tables):
    panels = tables[0].shape[1]
    clusters = panels // CL
    places = len(tables) * clusters
    whole = pl.BlockSpec(memory_space=pltpu.VMEM)
    return pl.pallas_call(
        functools.partial(pair_kernel, clusters),
        out_shape=jax.ShapeDtypeStruct((2, panels), f32),
        in_specs=[whole] * len(tables),
        out_specs=whole,
        scratch_shapes=[
            pltpu.VMEM((8, CL), jnp.int32),
            pltpu.SMEM((8, CL), jnp.int32),
            pltpu.SemaphoreType.DMA,
            pltpu.SMEM((8 * CL + 8,), jnp.int32),
            pltpu.VMEM((clusters + 1, QUAD * CL, CL), bf16),
            pltpu.VMEM((places, DEPTH, QUAD * CL), bf16),
            pltpu.VMEM((places, 16, CL), f32),
            pltpu.VMEM((clusters + 1, QUAD * CL, CL), f32),
            pltpu.VMEM((clusters + 1, 2 * CL, CL), f32),
        ],
        compiler_params=pltpu.CompilerParams(vmem_limit_bytes=56 * 1024 * 1024),
        name="pairs",
    )(*tables)


def pack_kernel(points, weights, density, near_pairs, gap_pairs, out):
    for q in range(QUAD):
        for c in range(3):
            out[4 * q + c : 4 * q + c + 1, :] = points[c, q : q + 1, :]
        out[4 * q + 3 : 4 * q + 4, :] = weights[q : q + 1, :]
    out[12:14, :] = density[...]
    out[14:16, :] = jnp.zeros((2, out.shape[1]), f32)
    for k in range(3):
        out[14:15, k * CL : k * CL + near_pairs.shape[1]] = near_pairs[k : k + 1, :].astype(f32)
        out[15:16, k * CL : k * CL + gap_pairs.shape[1]] = gap_pairs[k : k + 1, :].astype(f32)


def packed(points, weights, density, near_pairs, gap_pairs):
    whole = pl.BlockSpec(memory_space=pltpu.VMEM)
    return pl.pallas_call(
        pack_kernel,
        out_shape=jax.ShapeDtypeStruct((16, points.shape[2]), f32),
        in_specs=[whole] * 5,
        out_specs=whole,
        name="pack",
    )(points, weights, density, near_pairs, gap_pairs)


near_partners = (
    lambda i: i ^ 1,
    lambda i: ((i + 1) ^ 1) - 1,
    lambda i: i ^ 2,
    lambda i: ((i + 2) ^ 2) - 2,
)


def swapped(block, axis, partner):
    size = lax.axis_size(axis)
    route = [(i, partner(i)) for i in range(size) if 0 <= partner(i) < size]
    return lax.ppermute(block, axis, route)


def per_device(points, weights, density, near_pairs, gap_pairs):
    local = packed(points, weights, density, near_pairs, gap_pairs)
    tables = [local] + [swapped(local, "dev", partner) for partner in near_partners]
    tables += [swapped(local, "section", lambda i, k=k: i ^ k) for k in (1, 2, 3)]
    return pair_sums(tables)


def solution(mesh):
    placed = (
        P(None, None, ("section", "dev")),
        P(None, ("section", "dev")),
        P(None, ("section", "dev")),
        P(None, ("section", "dev")),
        P(None, ("section", "dev")),
    )
    return jax.shard_map(
        per_device,
        mesh=mesh,
        in_specs=placed,
        out_specs=P(None, ("section", "dev")),
        check_vma=False,
    )
```

```python
import functools
import math

import jax
import jax.numpy as jnp
from jax import lax
from jax.experimental import pallas as pl
from jax.experimental.pallas import tpu as pltpu
from jax.sharding import PartitionSpec as P

CL = 128
QUAD = 3
DEPTH = 48
TURNED = 64
UNROLL = 8
TABLE_ORDER = (4, 3, 7, 5, 6, 2, 1)

smoothing = 0.02
green_scale = 0.25 / math.pi
f32 = jnp.float32
bf16 = jnp.bfloat16


def rounded(x, magic):
    return (x + magic) - magic


def row_ids(like):
    return lax.broadcasted_iota(jnp.int32, like.shape, 0)


def parts_of(tile, row_limit):
    rows = row_ids(tile)
    live = jnp.logical_and(lax.rem(rows, 4) < 3, rows < row_limit)
    x = jnp.where(live, tile, 0.0)
    high = rounded(x, 49152.0)
    rest = x - high
    mid = rounded(rest, 96.0)
    low = rounded(rest - mid, 0.1875)
    rest = mid + low
    sq_high = high * high
    sq_rest = rest * (high + high + rest)

    def row_sum(v):
        u = v + pltpu.roll(v, 7, 0)
        return u + pltpu.roll(u, 6, 0)

    return high, mid, low, row_sum(sq_high), row_sum(sq_rest)


def square_parts(sum_high, sum_rest):
    rows = row_ids(sum_high)
    upper = rows < 4
    v = jnp.where(upper, sum_high, sum_rest)
    one = rounded(v, jnp.where(upper, 196608.0, 768.0))
    rest = v - one
    two = rounded(rest, jnp.where(upper, 768.0, 3.0))
    three = rest - two
    place = lax.rem(rows, 4)
    return jnp.where(place == 0, one, jnp.where(place == 1, two, jnp.where(place == 2, three, 0.0)))


def point_features(tile0, tile1):
    h0, m0, l0, sh0, sr0 = parts_of(tile0, 8)
    h1, m1, l1, sh1, sr1 = parts_of(tile1, 3)

    def spread(v, row):
        return jnp.broadcast_to(v[row : row + 1], v.shape)

    turn = lambda v: pltpu.roll(v, 4, 0)
    return (
        (h0, m0, l0, turn(l0), spread(sh0, 0), spread(sr0, 0)),
        (turn(h0), turn(m0), turn(l0), l0, spread(sh0, 4), spread(sr0, 4)),
        (h1, m1, l1, turn(l1), spread(sh1, 0), spread(sr1, 0)),
    )


def right_features(tile0, tile1):
    rows = row_ids(tile0)
    out = []
    for high, mid, low, low_turned, sum_high, sum_rest in point_features(tile0, tile1):
        ones = jnp.where(rows < 6, 1.0, 0.0)
        g0 = jnp.where(rows < 3, high, jnp.where(rows < 6, ones, pltpu.roll(mid, 6, 0)))
        g1 = square_parts(sum_high, sum_rest + smoothing * smoothing)
        g1 = jnp.where(rows == 7, pltpu.roll(mid, 5, 0), g1)
        g4 = jnp.where(rows < 4, mid, low_turned)
        out.append(jnp.concatenate([g0, g1, g0, g0, g4, g4], 0).astype(bf16))
    return out


def left_features(tile0, tile1):
    rows = row_ids(tile0)
    out = []
    for high, mid, low, low_turned, sum_high, sum_rest in point_features(tile0, tile1):
        sq = square_parts(sum_high, sum_rest)
        sq_high = pltpu.roll(sq, 3, 0)
        sq_rest = pltpu.roll(sq, 7, 0)
        first = rows < 3
        mids = jnp.logical_and(rows >= 3, rows < 6)
        h2 = jnp.where(first, -2.0 * high, 0.0)
        m2 = jnp.where(first, -2.0 * mid, 0.0)
        l2 = jnp.where(first, -2.0 * low, 0.0)
        b0 = jnp.where(mids, sq_high, h2)
        b1 = jnp.where(lax.rem(rows, 4) < 3, 1.0, jnp.where(rows == 7, pltpu.roll(l2, 5, 0), 0.0))
        b3 = jnp.where(rows < 6, l2, pltpu.roll(l2, 6, 0))
        b2 = jnp.where(mids, sq_rest, m2)
        b4 = h2 + pltpu.roll(h2, 4, 0)
        b5 = m2 + pltpu.roll(m2, 4, 0)
        out.append(jnp.concatenate([b0, b1, b2, b3, b4, b5], 0))
    return out


def pair_codes(here, local, others, codes):
    def lists(table, row):
        return [table[row : row + 1, k * CL : (k + 1) * CL].astype(jnp.int32) for k in range(3)]

    low5 = lambda v: jnp.bitwise_and(v, 31)
    up5 = lambda v: lax.shift_right_logical(v, 5)

    def coded(valid, here, slot, there):
        return jnp.where(valid, low5(here) + (slot * 32 + low5(there)) * 256, -1)

    first, second, listed = lists(local, 14)
    me = jnp.broadcast_to(up5(first[:, 0:1]), first.shape)
    my_dev, dev = low5(me), low5(up5(second))
    slot = jnp.full(first.shape, 4, jnp.int32)
    slot = jnp.where(dev == jnp.bitwise_xor(my_dev, 2), 3, slot)
    slot = jnp.where(dev == jnp.bitwise_xor(my_dev + 1, 1) - 1, 2, slot)
    slot = jnp.where(dev == jnp.bitwise_xor(my_dev, 1), 1, slot)
    slot = jnp.where(dev == my_dev, 0, slot)
    inside = slot == 0
    if here:
        codes[0:1, :] = coded(jnp.logical_and(listed > 0, inside), first, 0, second)
        inside = jnp.logical_and(inside, first != second)
        codes[1:2, :] = coded(jnp.logical_and(listed > 0, inside), second, 0, first)
        return
    codes[0:1, :] = coded(jnp.logical_and(listed > 0, slot > 0), first, slot, second)
    for slot_in in range(1, 5):
        first, second, listed = lists(others[slot_in - 1], 14)
        valid = jnp.logical_and(listed > 0, up5(second) == me)
        codes[slot_in : slot_in + 1, :] = coded(valid, second, slot_in, first)
    first, second, listed = lists(local, 15)
    slot = 4 + jnp.bitwise_xor(up5(me), up5(up5(second)))
    row = coded(listed > 0, first, slot, second)
    lanes = lax.broadcasted_iota(jnp.int32, row.shape, 1)
    for slot_in in range(5, 8):
        first, second, listed = lists(others[slot_in - 1], 15)
        valid = jnp.logical_and(listed > 0, up5(second) == me)
        incoming = coded(valid, second, slot_in, first)
        row = jnp.where(lanes < 32 * (slot_in - 4), row, pltpu.roll(incoming, 32 * (slot_in - 4), 1))
    codes[5:6, :] = row


WIDE = 4


def pair_kernel(here, clusters, *refs):
    tables = refs[:1] if here else refs[:8]
    local = tables[0]
    refs = refs[len(tables) :]
    if not here:
        tables = [local] + [tables[1 + TABLE_ORDER.index(slot)] for slot in range(1, 8)]
    if here:
        out, left_kept, wide_kept = refs[:3]
    else:
        partial, left_kept, wide_kept, out = refs[:4]
    refs = refs[3 if here else 4 :]
    codes, codes_smem, sems, todo, left, right, raw, wide_w, acc = refs
    used = tables if here else tables[1:]
    base = 0 if here else clusters

    pair_codes(here, local, tables[1:], codes)
    lists_copy = pltpu.make_async_copy(codes, codes_smem, sems.at[0])
    lists_copy.start()
    ends = (left.at[0:clusters], left_kept), (wide_w.at[0:clusters], wide_kept)
    if not here:
        ends = [(b, a) for a, b in ends]
    kept_copies = [pltpu.make_async_copy(a, b, sems.at[1 + k]) for k, (a, b) in enumerate(ends)]

    def prepare_left(n, carry):
        for u in range(2):
            c = n * 2 + u
            lanes = pl.ds(pl.multiple_of(c * CL, CL), CL)
            tile0, tile1 = local[0:8, lanes], local[8:16, lanes]
            weight_rows = (tile0[3:4], tile0[7:8], tile1[3:4])
            for q, block in enumerate(left_features(tile0, tile1)):
                weight = jnp.broadcast_to(weight_rows[q] * green_scale, (8, CL))
                block = jnp.concatenate([block, weight, jnp.zeros((TURNED - DEPTH - 8, CL), f32)], 0)
                turned = jnp.transpose(block)
                left[c, q * CL : (q + 1) * CL, 0:TURNED] = turned.astype(bf16)
                wide_w[c, q * CL : (q + 1) * CL, :] = jnp.broadcast_to(turned[:, DEPTH : DEPTH + 1], (CL, CL))
        return carry

    if here:
        lax.fori_loop(0, clusters // 2, prepare_left, 0)
    for copy in kept_copies:
        copy.start()
    lists_copy.wait()

    steps = clusters // WIDE
    rows_of_codes = 2 if here else 6
    count = 0
    for table in range(len(used)):

        def prepare_right(n, count):
            lanes = pl.ds(pl.multiple_of(n * (WIDE * CL), WIDE * CL), WIDE * CL)
            tile0, tile1 = used[table][0:8, lanes], used[table][8:16, lanes]
            blocks = right_features(tile0, tile1)
            for u in range(WIDE):
                place = table * clusters + n * WIDE + u
                cut = slice(u * CL, (u + 1) * CL)
                for q in range(QUAD):
                    right[place, :, q * CL : (q + 1) * CL] = blocks[q][:, cut]
                raw[place, 0:8, :] = tile0[:, cut]
                raw[place, 8:16, :] = tile1[:, cut]
                if table == 0:
                    acc[n * WIDE + u] = jnp.zeros((2 * CL, CL), f32)
            rows = range(2) if here else ([table] if table < 6 else [])
            for row in rows:
                for u in range(CL // 8):
                    code = codes_smem[row, n * (CL // 8) + u]
                    todo[count] = code
                    count = count + (code >= 0).astype(jnp.int32)
            return count

        count = lax.fori_loop(0, steps, prepare_right, count)
    for extra in range(UNROLL - 1):
        todo[count + extra] = clusters + base * 256
    if not here:
        for copy in kept_copies:
            copy.wait()

    def tile_of(i, j):
        weight_b = (raw[j, 3:4, :], raw[j, 7:8, :], raw[j, 11:12, :])
        far = right[j]
        total = None
        for p in range(QUAD):
            near = left[i, p * CL : (p + 1) * CL, 0:DEPTH]
            dist = jnp.dot(near, far, preferred_element_type=f32)
            row = None
            for q in range(QUAD):
                term = weight_b[q] * lax.rsqrt(dist[:, q * CL : (q + 1) * CL])
                row = term if row is None else row + term
            row = row * wide_w[i, p * CL : (p + 1) * CL, :]
            total = row if total is None else total + row
        return total

    def group(g, carry):
        done = []
        for u in range(UNROLL):
            code = todo[g * UNROLL + u]
            i = jnp.bitwise_and(code, 255)
            j = lax.shift_right_logical(code, 8) - base
            done.append((i, j, tile_of(i, j)))
        for i, j, tile in done:
            for r in range(2):
                acc[i, r * CL : (r + 1) * CL, :] += tile * raw[j, 12 + r : 13 + r, :]
        return carry

    lax.fori_loop(0, lax.div(count + UNROLL - 1, UNROLL), group, 0)

    def finish(n, carry):
        for u in range(4):
            c = n * 4 + u
            lanes = pl.ds(pl.multiple_of(c * CL, CL), CL)
            value = acc[c]
            high = value.astype(bf16)
            low = (value - high.astype(f32)).astype(bf16)
            both = jnp.concatenate([high, low], 1)
            ones = jnp.ones((8, 2 * CL), bf16)
            sums = lax.dot_general(ones, both, (((1,), (1,)), ((), ())), preferred_element_type=f32)
            for r in range(2):
                line = sums[0:1, r * CL : (r + 1) * CL]
                if not here:
                    line = line + partial[r : r + 1, lanes]
                out[r : r + 1, lanes] = line
        return carry

    lax.fori_loop(0, clusters // 4, finish, 0)
    if here:
        for copy in kept_copies:
            copy.wait()


def pair_sums(tables, kept=None):
    here = kept is None
    panels = tables[0].shape[1]
    clusters = panels // CL
    places = (1 if here else len(tables) - 1) * clusters
    whole = pl.BlockSpec(memory_space=pltpu.VMEM)
    far = pl.BlockSpec(memory_space=pl.ANY)
    result = jax.ShapeDtypeStruct((2, panels), f32)
    left = jax.ShapeDtypeStruct((clusters, QUAD * CL, CL), bf16)
    wide = jax.ShapeDtypeStruct((clusters, QUAD * CL, CL), f32)
    return pl.pallas_call(
        functools.partial(pair_kernel, here, clusters),
        out_shape=[result, left, wide] if here else result,
        in_specs=[whole] * len(tables) + ([] if here else [whole, far, far]),
        out_specs=[whole, far, far] if here else whole,
        scratch_shapes=[
            pltpu.VMEM((8, CL), jnp.int32),
            pltpu.SMEM((8, CL), jnp.int32),
            pltpu.SemaphoreType.DMA((3,)),
            pltpu.SMEM((8 * CL + UNROLL,), jnp.int32),
            pltpu.VMEM((clusters + 1, QUAD * CL, CL), bf16),
            pltpu.VMEM((places, DEPTH, QUAD * CL), bf16),
            pltpu.VMEM((places, 16, CL), f32),
            pltpu.VMEM((clusters + 1, QUAD * CL, CL), f32),
            pltpu.VMEM((clusters + 1, 2 * CL, CL), f32),
        ],
        compiler_params=pltpu.CompilerParams(vmem_limit_bytes=(30 if here else 40) * 1024 * 1024),
        cost_estimate=pl.CostEstimate(
            flops=2_000_000_000, bytes_accessed=(40 if here else 80) * 1024 * 1024, transcendentals=10_000_000
        ),
        name="pairs_here" if here else "pairs_across",
    )(*tables, *(kept or ()))


def pack_kernel(points, weights, density, near_pairs, gap_pairs, out):
    for q in range(QUAD):
        for c in range(3):
            out[4 * q + c : 4 * q + c + 1, :] = points[c, q : q + 1, :]
        out[4 * q + 3 : 4 * q + 4, :] = weights[q : q + 1, :]
    out[12:14, :] = density[...]
    out[14:16, :] = jnp.zeros((2, out.shape[1]), f32)
    for k in range(3):
        out[14:15, k * CL : k * CL + near_pairs.shape[1]] = near_pairs[k : k + 1, :].astype(f32)
        out[15:16, k * CL : k * CL + gap_pairs.shape[1]] = gap_pairs[k : k + 1, :].astype(f32)


def packed(points, weights, density, near_pairs, gap_pairs):
    whole = pl.BlockSpec(memory_space=pltpu.VMEM)
    return pl.pallas_call(
        pack_kernel,
        out_shape=jax.ShapeDtypeStruct((16, points.shape[2]), f32),
        in_specs=[whole] * 5,
        out_specs=whole,
        name="pack",
    )(points, weights, density, near_pairs, gap_pairs)


near_partners = (
    lambda i: i ^ 1,
    lambda i: ((i + 1) ^ 1) - 1,
    lambda i: i ^ 2,
    lambda i: ((i + 2) ^ 2) - 2,
)


def swapped(block, axis, partner):
    size = lax.axis_size(axis)
    route = [(i, partner(i)) for i in range(size) if 0 <= partner(i) < size]
    return lax.ppermute(block, axis, route)


def per_device(points, weights, density, near_pairs, gap_pairs):
    local = packed(points, weights, density, near_pairs, gap_pairs)
    tables = [local]
    for slot in TABLE_ORDER:
        if slot > 4:
            tables.append(swapped(local, "section", lambda i, k=slot - 4: i ^ k))
        else:
            tables.append(swapped(local, "dev", near_partners[slot - 1]))
    kept = pair_sums(tables[:1])
    return pair_sums(tables, kept)


def solution(mesh):
    placed = (
        P(None, None, ("section", "dev")),
        P(None, ("section", "dev")),
        P(None, ("section", "dev")),
        P(None, ("section", "dev")),
        P(None, ("section", "dev")),
    )
    return jax.shard_map(
        per_device,
        mesh=mesh,
        in_specs=placed,
        out_specs=P(None, ("section", "dev")),
        check_vma=False,
    )
```

```python
import functools
import math

import jax
import jax.numpy as jnp
from jax import lax
from jax.experimental import pallas as pl
from jax.experimental.pallas import tpu as pltpu
from jax.sharding import PartitionSpec as P

CL = 128
QUAD = 3
DEPTH = 48
TURNED = 64
UNROLL = 8
TABLE_ORDER = (4, 3, 7, 5, 6, 2, 1)

smoothing = 0.02
green_scale = 0.25 / math.pi
f32 = jnp.float32
bf16 = jnp.bfloat16


def rounded(x, magic):
    return (x + magic) - magic


def row_ids(like):
    return lax.broadcasted_iota(jnp.int32, like.shape, 0)


def parts_of(tile, row_limit):
    rows = row_ids(tile)
    live = jnp.logical_and(lax.rem(rows, 4) < 3, rows < row_limit)
    x = jnp.where(live, tile, 0.0)
    high = rounded(x, 49152.0)
    rest = x - high
    mid = rounded(rest, 96.0)
    low = rounded(rest - mid, 0.1875)
    rest = mid + low
    sq_high = high * high
    sq_rest = rest * (high + high + rest)

    def row_sum(v):
        u = v + pltpu.roll(v, 7, 0)
        return u + pltpu.roll(u, 6, 0)

    return high, mid, low, row_sum(sq_high), row_sum(sq_rest)


def square_parts(sum_high, sum_rest):
    rows = row_ids(sum_high)
    upper = rows < 4
    v = jnp.where(upper, sum_high, sum_rest)
    one = rounded(v, jnp.where(upper, 196608.0, 768.0))
    rest = v - one
    two = rounded(rest, jnp.where(upper, 768.0, 3.0))
    three = rest - two
    place = lax.rem(rows, 4)
    return jnp.where(place == 0, one, jnp.where(place == 1, two, jnp.where(place == 2, three, 0.0)))


def point_features(tile0, tile1):
    h0, m0, l0, sh0, sr0 = parts_of(tile0, 8)
    h1, m1, l1, sh1, sr1 = parts_of(tile1, 3)

    def spread(v, row):
        return jnp.broadcast_to(v[row : row + 1], v.shape)

    turn = lambda v: pltpu.roll(v, 4, 0)
    return (
        (h0, m0, l0, turn(l0), spread(sh0, 0), spread(sr0, 0)),
        (turn(h0), turn(m0), turn(l0), l0, spread(sh0, 4), spread(sr0, 4)),
        (h1, m1, l1, turn(l1), spread(sh1, 0), spread(sr1, 0)),
    )


def right_features(tile0, tile1):
    rows = row_ids(tile0)
    out = []
    for high, mid, low, low_turned, sum_high, sum_rest in point_features(tile0, tile1):
        ones = jnp.where(rows < 6, 1.0, 0.0)
        g0 = jnp.where(rows < 3, high, jnp.where(rows < 6, ones, pltpu.roll(mid, 6, 0)))
        g1 = square_parts(sum_high, sum_rest + smoothing * smoothing)
        g1 = jnp.where(rows == 7, pltpu.roll(mid, 5, 0), g1)
        g4 = jnp.where(rows < 4, mid, low_turned)
        out.append(jnp.concatenate([g0, g1, g0, g0, g4, g4], 0).astype(bf16))
    return out


def left_features(tile0, tile1):
    rows = row_ids(tile0)
    out = []
    for high, mid, low, low_turned, sum_high, sum_rest in point_features(tile0, tile1):
        sq = square_parts(sum_high, sum_rest)
        sq_high = pltpu.roll(sq, 3, 0)
        sq_rest = pltpu.roll(sq, 7, 0)
        first = rows < 3
        mids = jnp.logical_and(rows >= 3, rows < 6)
        h2 = jnp.where(first, -2.0 * high, 0.0)
        m2 = jnp.where(first, -2.0 * mid, 0.0)
        l2 = jnp.where(first, -2.0 * low, 0.0)
        b0 = jnp.where(mids, sq_high, h2)
        b1 = jnp.where(lax.rem(rows, 4) < 3, 1.0, jnp.where(rows == 7, pltpu.roll(l2, 5, 0), 0.0))
        b3 = jnp.where(rows < 6, l2, pltpu.roll(l2, 6, 0))
        b2 = jnp.where(mids, sq_rest, m2)
        b4 = h2 + pltpu.roll(h2, 4, 0)
        b5 = m2 + pltpu.roll(m2, 4, 0)
        out.append(jnp.concatenate([b0, b1, b2, b3, b4, b5], 0))
    return out


def pair_codes(here, local, others, codes):
    def lists(table, row):
        return [table[row : row + 1, k * CL : (k + 1) * CL].astype(jnp.int32) for k in range(3)]

    low5 = lambda v: jnp.bitwise_and(v, 31)
    up5 = lambda v: lax.shift_right_logical(v, 5)

    def coded(valid, here, slot, there):
        return jnp.where(valid, low5(here) + (slot * 32 + low5(there)) * 256, -1)

    first, second, listed = lists(local, 14)
    me = jnp.broadcast_to(up5(first[:, 0:1]), first.shape)
    my_dev, dev = low5(me), low5(up5(second))
    slot = jnp.full(first.shape, 4, jnp.int32)
    slot = jnp.where(dev == jnp.bitwise_xor(my_dev, 2), 3, slot)
    slot = jnp.where(dev == jnp.bitwise_xor(my_dev + 1, 1) - 1, 2, slot)
    slot = jnp.where(dev == jnp.bitwise_xor(my_dev, 1), 1, slot)
    slot = jnp.where(dev == my_dev, 0, slot)
    inside = slot == 0
    if here:
        codes[0:1, :] = coded(jnp.logical_and(listed > 0, inside), first, 0, second)
        inside = jnp.logical_and(inside, first != second)
        codes[1:2, :] = coded(jnp.logical_and(listed > 0, inside), second, 0, first)
        return
    codes[0:1, :] = coded(jnp.logical_and(listed > 0, slot > 0), first, slot, second)
    for slot_in in range(1, 5):
        first, second, listed = lists(others[slot_in - 1], 14)
        valid = jnp.logical_and(listed > 0, up5(second) == me)
        codes[slot_in : slot_in + 1, :] = coded(valid, second, slot_in, first)
    first, second, listed = lists(local, 15)
    slot = 4 + jnp.bitwise_xor(up5(me), up5(up5(second)))
    row = coded(listed > 0, first, slot, second)
    lanes = lax.broadcasted_iota(jnp.int32, row.shape, 1)
    for slot_in in range(5, 8):
        first, second, listed = lists(others[slot_in - 1], 15)
        valid = jnp.logical_and(listed > 0, up5(second) == me)
        incoming = coded(valid, second, slot_in, first)
        row = jnp.where(lanes < 32 * (slot_in - 4), row, pltpu.roll(incoming, 32 * (slot_in - 4), 1))
    codes[5:6, :] = row


WIDE = 8


def pair_kernel(here, clusters, *refs):
    tables = refs[:1] if here else refs[:8]
    local = tables[0]
    refs = refs[len(tables) :]
    if not here:
        tables = [local] + [tables[1 + TABLE_ORDER.index(slot)] for slot in range(1, 8)]
    if here:
        left, wide_w, acc = refs[:3]
        refs = refs[3:]
    else:
        left, wide_w, _, out, acc = refs[:5]
        refs = refs[5:]
    codes, codes_smem, sem, todo, right, raw = refs
    used = tables if here else tables[1:]
    base = 0 if here else clusters

    pair_codes(here, local, tables[1:], codes)
    lists_copy = pltpu.make_async_copy(codes, codes_smem, sem)
    lists_copy.start()

    def prepare_left(n, carry):
        for u in range(WIDE):
            c = n * WIDE + u
            lanes = pl.ds(pl.multiple_of(c * CL, CL), CL)
            tile0, tile1 = local[0:8, lanes], local[8:16, lanes]
            weight_rows = (tile0[3:4], tile0[7:8], tile1[3:4])
            for q, block in enumerate(left_features(tile0, tile1)):
                weight = jnp.broadcast_to(weight_rows[q] * green_scale, (8, CL))
                block = jnp.concatenate([block, weight, jnp.zeros((TURNED - DEPTH - 8, CL), f32)], 0)
                turned = jnp.transpose(block)
                left[c, q * CL : (q + 1) * CL, 0:TURNED] = turned.astype(bf16)
                wide_w[c, q * CL : (q + 1) * CL, :] = jnp.broadcast_to(turned[:, DEPTH : DEPTH + 1], (CL, CL))
            acc[c] = jnp.zeros((2 * CL, CL), f32)
        return carry

    if here:
        lax.fori_loop(0, clusters // WIDE, prepare_left, 0)
    lists_copy.wait()

    steps = clusters // WIDE
    rows_of_codes = 2 if here else 6
    count = 0
    for table in range(len(used)):

        def prepare_right(n, count):
            lanes = pl.ds(pl.multiple_of(n * (WIDE * CL), WIDE * CL), WIDE * CL)
            tile0, tile1 = used[table][0:8, lanes], used[table][8:16, lanes]
            blocks = right_features(tile0, tile1)
            for u in range(WIDE):
                place = table * clusters + n * WIDE + u
                cut = slice(u * CL, (u + 1) * CL)
                for q in range(QUAD):
                    right[place, :, q * CL : (q + 1) * CL] = blocks[q][:, cut]
                raw[place, 0:8, :] = tile0[:, cut]
                raw[place, 8:16, :] = tile1[:, cut]
            rows = range(2) if here else ([table] if table < 6 else [])
            for row in rows:
                for u in range(CL // steps):
                    code = codes_smem[row, n * (CL // steps) + u]
                    todo[count] = code
                    count = count + (code >= 0).astype(jnp.int32)
            return count

        count = lax.fori_loop(0, steps, prepare_right, count)
    for extra in range(UNROLL - 1):
        todo[count + extra] = clusters + base * 256

    def tile_of(i, j):
        weight_b = (raw[j, 3:4, :], raw[j, 7:8, :], raw[j, 11:12, :])
        far = right[j]
        total = None
        for p in range(QUAD):
            near = left[i, p * CL : (p + 1) * CL, 0:DEPTH]
            dist = jnp.dot(near, far, preferred_element_type=f32)
            row = None
            for q in range(QUAD):
                term = weight_b[q] * lax.rsqrt(dist[:, q * CL : (q + 1) * CL])
                row = term if row is None else row + term
            row = row * wide_w[i, p * CL : (p + 1) * CL, :]
            total = row if total is None else total + row
        return total

    def group(g, carry):
        done = []
        for u in range(UNROLL):
            code = todo[g * UNROLL + u]
            i = jnp.bitwise_and(code, 255)
            j = lax.shift_right_logical(code, 8) - base
            done.append((i, j, tile_of(i, j)))
        for i, j, tile in done:
            for r in range(2):
                acc[i, r * CL : (r + 1) * CL, :] += tile * raw[j, 12 + r : 13 + r, :]
        return carry

    lax.fori_loop(0, lax.div(count + UNROLL - 1, UNROLL), group, 0)

    if here:
        return

    def finish(n, carry):
        for u in range(4):
            c = n * 4 + u
            lanes = pl.ds(pl.multiple_of(c * CL, CL), CL)
            value = acc[c]
            high = value.astype(bf16)
            low = (value - high.astype(f32)).astype(bf16)
            both = jnp.concatenate([high, low], 1)
            ones = jnp.ones((8, 2 * CL), bf16)
            sums = lax.dot_general(ones, both, (((1,), (1,)), ((), ())), preferred_element_type=f32)
            for r in range(2):
                out[r : r + 1, lanes] = sums[0:1, r * CL : (r + 1) * CL]
        return carry

    lax.fori_loop(0, clusters // 4, finish, 0)


def pair_sums(tables, kept=None):
    here = kept is None
    panels = tables[0].shape[1]
    clusters = panels // CL
    places = (1 if here else len(tables) - 1) * clusters
    whole = pl.BlockSpec(memory_space=pltpu.VMEM)
    result = jax.ShapeDtypeStruct((2, panels), f32)
    left = jax.ShapeDtypeStruct((clusters + 1, QUAD * CL, CL), bf16)
    wide = jax.ShapeDtypeStruct((clusters + 1, QUAD * CL, CL), f32)
    acc = jax.ShapeDtypeStruct((clusters + 1, 2 * CL, CL), f32)
    return pl.pallas_call(
        functools.partial(pair_kernel, here, clusters),
        out_shape=[left, wide, acc] if here else [result, acc],
        in_specs=[whole] * (len(tables) + (0 if here else 3)),
        out_specs=[whole] * (3 if here else 2),
        input_output_aliases={} if here else {len(tables) + 2: 1},
        scratch_shapes=[
            pltpu.VMEM((8, CL), jnp.int32),
            pltpu.SMEM((8, CL), jnp.int32),
            pltpu.SemaphoreType.DMA,
            pltpu.SMEM((8 * CL + UNROLL,), jnp.int32),
            pltpu.VMEM((places, DEPTH, QUAD * CL), bf16),
            pltpu.VMEM((places, 16, CL), f32),
        ],
        compiler_params=pltpu.CompilerParams(vmem_limit_bytes=32 * 1024 * 1024),
        cost_estimate=pl.CostEstimate(
            flops=2_000_000_000, bytes_accessed=(40 if here else 80) * 1024 * 1024, transcendentals=10_000_000
        ),
        name="pairs_here" if here else "pairs_across",
    )(*tables, *(kept or ()))


def pack_kernel(*refs):
    sent, out = refs[5:7]
    points, weights, density, near_pairs, gap_pairs = refs[7:12]
    copies = [pltpu.make_async_copy(refs[k], refs[7 + k], refs[12].at[k]) for k in range(5)]
    for copy in copies:
        copy.start()
    for copy in copies:
        copy.wait()
    for q in range(QUAD):
        for c in range(3):
            out[4 * q + c : 4 * q + c + 1, :] = points[c, q : q + 1, :]
        out[4 * q + 3 : 4 * q + 4, :] = weights[q : q + 1, :]
    out[12:14, :] = density[...]
    out[14:16, :] = jnp.zeros((2, out.shape[1]), f32)
    for k in range(3):
        out[14:15, k * CL : k * CL + near_pairs.shape[1]] = near_pairs[k : k + 1, :].astype(f32)
        out[15:16, k * CL : k * CL + gap_pairs.shape[1]] = gap_pairs[k : k + 1, :].astype(f32)
    sent[...] = out[...]


def packed(points, weights, density, near_pairs, gap_pairs):
    whole = pl.BlockSpec(memory_space=pltpu.VMEM)
    return pl.pallas_call(
        pack_kernel,
        out_shape=[jax.ShapeDtypeStruct((16, points.shape[2]), f32)] * 2,
        in_specs=[pl.BlockSpec(memory_space=pltpu.HBM)] * 5,
        out_specs=[whole] * 2,
        scratch_shapes=[pltpu.VMEM(x.shape, x.dtype) for x in (points, weights, density, near_pairs, gap_pairs)]
        + [pltpu.SemaphoreType.DMA((5,))],
        compiler_params=pltpu.CompilerParams(vmem_limit_bytes=8 * 1024 * 1024),
        name="pack",
    )(*[pltpu.with_memory_space_constraint(x, pltpu.HBM) for x in (points, weights, density, near_pairs, gap_pairs)])


near_partners = (
    lambda i: i ^ 1,
    lambda i: ((i + 1) ^ 1) - 1,
    lambda i: i ^ 2,
    lambda i: ((i + 2) ^ 2) - 2,
)


def swapped(block, axis, partner):
    size = lax.axis_size(axis)
    route = [(i, partner(i)) for i in range(size) if 0 <= partner(i) < size]
    return lax.ppermute(block, axis, route)


def per_device(points, weights, density, near_pairs, gap_pairs):
    sent, local = packed(points, weights, density, near_pairs, gap_pairs)
    tables = [local]
    for slot in TABLE_ORDER:
        if slot > 4:
            tables.append(swapped(sent, "section", lambda i, k=slot - 4: i ^ k))
        else:
            tables.append(swapped(sent, "dev", near_partners[slot - 1]))
    kept = pair_sums(tables[:1])
    return pair_sums(tables, kept)[0]


def solution(mesh):
    placed = (
        P(None, None, ("section", "dev")),
        P(None, ("section", "dev")),
        P(None, ("section", "dev")),
        P(None, ("section", "dev")),
        P(None, ("section", "dev")),
    )
    return jax.shard_map(
        per_device,
        mesh=mesh,
        in_specs=placed,
        out_specs=P(None, ("section", "dev")),
        check_vma=False,
    )
```

```python
import functools
import math

import jax
import jax.numpy as jnp
from jax import lax
from jax.experimental import pallas as pl
from jax.experimental.pallas import tpu as pltpu
from jax.sharding import PartitionSpec as P

CL = 128
QUAD = 3
DEPTH = 48
TURNED = 64
UNROLL = 8
TABLE_ORDER = (4, 3, 7, 5, 6, 2, 1)

smoothing = 0.02
green_scale = 0.25 / math.pi
f32 = jnp.float32
bf16 = jnp.bfloat16


def rounded(x, magic):
    return (x + magic) - magic


def row_ids(like):
    return lax.broadcasted_iota(jnp.int32, like.shape, 0)


def parts_of(tile, row_limit):
    rows = row_ids(tile)
    live = jnp.logical_and(lax.rem(rows, 4) < 3, rows < row_limit)
    x = jnp.where(live, tile, 0.0)
    high = rounded(x, 49152.0)
    rest = x - high
    mid = rounded(rest, 96.0)
    low = rounded(rest - mid, 0.1875)
    rest = mid + low
    sq_high = high * high
    sq_rest = rest * (high + high + rest)

    def row_sum(v):
        u = v + pltpu.roll(v, 7, 0)
        return u + pltpu.roll(u, 6, 0)

    return high, mid, low, row_sum(sq_high), row_sum(sq_rest)


def square_parts(sum_high, sum_rest):
    rows = row_ids(sum_high)
    upper = rows < 4
    v = jnp.where(upper, sum_high, sum_rest)
    one = rounded(v, jnp.where(upper, 196608.0, 768.0))
    rest = v - one
    two = rounded(rest, jnp.where(upper, 768.0, 3.0))
    three = rest - two
    place = lax.rem(rows, 4)
    return jnp.where(place == 0, one, jnp.where(place == 1, two, jnp.where(place == 2, three, 0.0)))


def point_features(tile0, tile1):
    h0, m0, l0, sh0, sr0 = parts_of(tile0, 8)
    h1, m1, l1, sh1, sr1 = parts_of(tile1, 3)

    def spread(v, row):
        return jnp.broadcast_to(v[row : row + 1], v.shape)

    turn = lambda v: pltpu.roll(v, 4, 0)
    return (
        (h0, m0, l0, turn(l0), spread(sh0, 0), spread(sr0, 0)),
        (turn(h0), turn(m0), turn(l0), l0, spread(sh0, 4), spread(sr0, 4)),
        (h1, m1, l1, turn(l1), spread(sh1, 0), spread(sr1, 0)),
    )


def right_features(tile0, tile1):
    rows = row_ids(tile0)
    out = []
    for high, mid, low, low_turned, sum_high, sum_rest in point_features(tile0, tile1):
        ones = jnp.where(rows < 6, 1.0, 0.0)
        g0 = jnp.where(rows < 3, high, jnp.where(rows < 6, ones, pltpu.roll(mid, 6, 0)))
        g1 = square_parts(sum_high, sum_rest + smoothing * smoothing)
        g1 = jnp.where(rows == 7, pltpu.roll(mid, 5, 0), g1)
        g4 = jnp.where(rows < 4, mid, low_turned)
        out.append(jnp.concatenate([g0, g1, g0, g0, g4, g4], 0).astype(bf16))
    return out


def left_features(tile0, tile1):
    rows = row_ids(tile0)
    out = []
    for high, mid, low, low_turned, sum_high, sum_rest in point_features(tile0, tile1):
        sq = square_parts(sum_high, sum_rest)
        sq_high = pltpu.roll(sq, 3, 0)
        sq_rest = pltpu.roll(sq, 7, 0)
        first = rows < 3
        mids = jnp.logical_and(rows >= 3, rows < 6)
        h2 = jnp.where(first, -2.0 * high, 0.0)
        m2 = jnp.where(first, -2.0 * mid, 0.0)
        l2 = jnp.where(first, -2.0 * low, 0.0)
        b0 = jnp.where(mids, sq_high, h2)
        b1 = jnp.where(lax.rem(rows, 4) < 3, 1.0, jnp.where(rows == 7, pltpu.roll(l2, 5, 0), 0.0))
        b3 = jnp.where(rows < 6, l2, pltpu.roll(l2, 6, 0))
        b2 = jnp.where(mids, sq_rest, m2)
        b4 = h2 + pltpu.roll(h2, 4, 0)
        b5 = m2 + pltpu.roll(m2, 4, 0)
        out.append(jnp.concatenate([b0, b1, b2, b3, b4, b5], 0))
    return out


def pair_codes(here, local, others, codes):
    def lists(table, row):
        return [table[row : row + 1, k * CL : (k + 1) * CL].astype(jnp.int32) for k in range(3)]

    low5 = lambda v: jnp.bitwise_and(v, 31)
    up5 = lambda v: lax.shift_right_logical(v, 5)

    def coded(valid, here, slot, there):
        return jnp.where(valid, low5(here) + (slot * 32 + low5(there)) * 256, -1)

    first, second, listed = lists(local, 14)
    me = jnp.broadcast_to(up5(first[:, 0:1]), first.shape)
    my_dev, dev = low5(me), low5(up5(second))
    slot = jnp.full(first.shape, 4, jnp.int32)
    slot = jnp.where(dev == jnp.bitwise_xor(my_dev, 2), 3, slot)
    slot = jnp.where(dev == jnp.bitwise_xor(my_dev + 1, 1) - 1, 2, slot)
    slot = jnp.where(dev == jnp.bitwise_xor(my_dev, 1), 1, slot)
    slot = jnp.where(dev == my_dev, 0, slot)
    inside = slot == 0
    if here:
        codes[0:1, :] = coded(jnp.logical_and(listed > 0, inside), first, 0, second)
        inside = jnp.logical_and(inside, first != second)
        codes[1:2, :] = coded(jnp.logical_and(listed > 0, inside), second, 0, first)
        return
    codes[0:1, :] = coded(jnp.logical_and(listed > 0, slot > 0), first, slot, second)
    for slot_in in range(1, 5):
        first, second, listed = lists(others[slot_in - 1], 14)
        valid = jnp.logical_and(listed > 0, up5(second) == me)
        codes[slot_in : slot_in + 1, :] = coded(valid, second, slot_in, first)
    first, second, listed = lists(local, 15)
    slot = 4 + jnp.bitwise_xor(up5(me), up5(up5(second)))
    row = coded(listed > 0, first, slot, second)
    lanes = lax.broadcasted_iota(jnp.int32, row.shape, 1)
    for slot_in in range(5, 8):
        first, second, listed = lists(others[slot_in - 1], 15)
        valid = jnp.logical_and(listed > 0, up5(second) == me)
        incoming = coded(valid, second, slot_in, first)
        row = jnp.where(lanes < 32 * (slot_in - 4), row, pltpu.roll(incoming, 32 * (slot_in - 4), 1))
    codes[5:6, :] = row


WIDE = 8


def pair_kernel(here, clusters, *refs):
    tables = refs[:1] if here else refs[:8]
    local = tables[0]
    refs = refs[len(tables) :]
    if not here:
        tables = [local] + [tables[1 + TABLE_ORDER.index(slot)] for slot in range(1, 8)]
    if here:
        left, wide_w, acc = refs[:3]
        refs = refs[3:]
    else:
        left, wide_w, _, out, acc = refs[:5]
        refs = refs[5:]
    codes, codes_smem, sem, todo, right, raw = refs
    used = tables if here else tables[1:]
    base = 0 if here else clusters

    pair_codes(here, local, tables[1:], codes)
    lists_copy = pltpu.make_async_copy(codes, codes_smem, sem)
    lists_copy.start()

    def prepare_left(n, carry):
        for u in range(WIDE):
            c = n * WIDE + u
            lanes = pl.ds(pl.multiple_of(c * CL, CL), CL)
            tile0, tile1 = local[0:8, lanes], local[8:16, lanes]
            weight_rows = (tile0[3:4], tile0[7:8], tile1[3:4])
            for q, block in enumerate(left_features(tile0, tile1)):
                weight = jnp.broadcast_to(weight_rows[q] * green_scale, (8, CL))
                block = jnp.concatenate([block, weight, jnp.zeros((TURNED - DEPTH - 8, CL), f32)], 0)
                turned = jnp.transpose(block)
                left[c, q * CL : (q + 1) * CL, 0:TURNED] = turned.astype(bf16)
                wide_w[c, q * CL : (q + 1) * CL, :] = jnp.broadcast_to(turned[:, DEPTH : DEPTH + 1], (CL, CL))
            acc[c] = jnp.zeros((CL, CL), f32)
        return carry

    if here:
        lax.fori_loop(0, clusters // WIDE, prepare_left, 0)
    lists_copy.wait()

    steps = clusters // WIDE
    rows_of_codes = 2 if here else 6
    count = 0
    for table in range(len(used)):

        def prepare_right(n, count):
            lanes = pl.ds(pl.multiple_of(n * (WIDE * CL), WIDE * CL), WIDE * CL)
            tile0, tile1 = used[table][0:8, lanes], used[table][8:16, lanes]
            blocks = right_features(tile0, tile1)
            for u in range(WIDE):
                place = table * clusters + n * WIDE + u
                cut = slice(u * CL, (u + 1) * CL)
                for q in range(QUAD):
                    right[place, :, q * CL : (q + 1) * CL] = blocks[q][:, cut]
                raw[place, 0:8, :] = tile0[:, cut]
                raw[place, 8:16, :] = tile1[:, cut]
            rows = range(2) if here else ([table] if table < 6 else [])
            for row in rows:
                for u in range(CL // steps):
                    code = codes_smem[row, n * (CL // steps) + u]
                    todo[count] = code
                    count = count + (code >= 0).astype(jnp.int32)
            return count

        count = lax.fori_loop(0, steps, prepare_right, count)
    for extra in range(UNROLL - 1):
        todo[count + extra] = clusters + base * 256

    def tile_of(i, j):
        weight_b = (raw[j, 3:4, :], raw[j, 7:8, :], raw[j, 11:12, :])
        far = right[j]
        total = None
        for p in range(QUAD):
            near = left[i, p * CL : (p + 1) * CL, 0:DEPTH]
            dist = jnp.dot(near, far, preferred_element_type=f32)
            row = None
            for q in range(QUAD):
                term = weight_b[q] * lax.rsqrt(dist[:, q * CL : (q + 1) * CL])
                row = term if row is None else row + term
            row = row * wide_w[i, p * CL : (p + 1) * CL, :]
            total = row if total is None else total + row
        return total

    lower = lax.broadcasted_iota(jnp.int32, (1, CL), 1) < CL // 2

    def group(g, carry):
        done = []
        for u in range(UNROLL):
            code = todo[g * UNROLL + u]
            i = jnp.bitwise_and(code, 255)
            j = lax.shift_right_logical(code, 8) - base
            done.append((i, j, tile_of(i, j)))
        for i, j, tile in done:
            dens0, dens1 = raw[j, 12:13, :], raw[j, 13:14, :]
            same = tile * jnp.where(lower, dens0, dens1)
            other = tile * jnp.where(lower, dens1, dens0)
            acc[i] += same + pltpu.roll(other, CL // 2, 1)
        return carry

    lax.fori_loop(0, lax.div(count + UNROLL - 1, UNROLL), group, 0)

    if here:
        return

    rows = lax.broadcasted_iota(jnp.int32, (8, 2 * CL), 0)
    lanes_of = jnp.bitwise_and(lax.broadcasted_iota(jnp.int32, (8, 2 * CL), 1), CL - 1)
    chosen = jnp.where(rows == lanes_of // (CL // 2), 1.0, 0.0).astype(bf16)

    def finish(n, carry):
        for u in range(8):
            c = n * 8 + u
            lanes = pl.ds(pl.multiple_of(c * CL, CL), CL)
            value = acc[c]
            high = value.astype(bf16)
            low = (value - high.astype(f32)).astype(bf16)
            both = jnp.concatenate([high, low], 1)
            sums = lax.dot_general(chosen, both, (((1,), (1,)), ((), ())), preferred_element_type=f32)
            out[:, lanes] = sums[0:2]
        return carry

    lax.fori_loop(0, clusters // 8, finish, 0)


def pair_sums(tables, kept=None):
    here = kept is None
    panels = tables[0].shape[1]
    clusters = panels // CL
    places = (1 if here else len(tables) - 1) * clusters
    whole = pl.BlockSpec(memory_space=pltpu.VMEM)
    result = jax.ShapeDtypeStruct((2, panels), f32)
    left = jax.ShapeDtypeStruct((clusters + 1, QUAD * CL, CL), bf16)
    wide = jax.ShapeDtypeStruct((clusters + 1, QUAD * CL, CL), f32)
    acc = jax.ShapeDtypeStruct((clusters + 1, CL, CL), f32)
    return pl.pallas_call(
        functools.partial(pair_kernel, here, clusters),
        out_shape=[left, wide, acc] if here else [result, acc],
        in_specs=[whole] * (len(tables) + (0 if here else 3)),
        out_specs=[whole] * (3 if here else 2),
        input_output_aliases={} if here else {len(tables) + 2: 1},
        scratch_shapes=[
            pltpu.VMEM((8, CL), jnp.int32),
            pltpu.SMEM((8, CL), jnp.int32),
            pltpu.SemaphoreType.DMA,
            pltpu.SMEM((8 * CL + UNROLL,), jnp.int32),
            pltpu.VMEM((places, DEPTH, QUAD * CL), bf16),
            pltpu.VMEM((places, 16, CL), f32),
        ],
        compiler_params=pltpu.CompilerParams(vmem_limit_bytes=32 * 1024 * 1024),
        cost_estimate=pl.CostEstimate(
            flops=2_000_000_000, bytes_accessed=(40 if here else 80) * 1024 * 1024, transcendentals=10_000_000
        ),
        name="pairs_here" if here else "pairs_across",
    )(*tables, *(kept or ()))


def pack_kernel(*refs):
    sent, out = refs[5:7]
    points, weights, density, near_pairs, gap_pairs = refs[7:12]
    copies = [pltpu.make_async_copy(refs[k], refs[7 + k], refs[12].at[k]) for k in range(5)]
    for copy in copies:
        copy.start()
    for copy in copies:
        copy.wait()
    for q in range(QUAD):
        for c in range(3):
            out[4 * q + c : 4 * q + c + 1, :] = points[c, q : q + 1, :]
        out[4 * q + 3 : 4 * q + 4, :] = weights[q : q + 1, :]
    out[12:14, :] = density[...]
    out[14:16, :] = jnp.zeros((2, out.shape[1]), f32)
    for k in range(3):
        out[14:15, k * CL : k * CL + near_pairs.shape[1]] = near_pairs[k : k + 1, :].astype(f32)
        out[15:16, k * CL : k * CL + gap_pairs.shape[1]] = gap_pairs[k : k + 1, :].astype(f32)
    sent[...] = out[...]


def packed(points, weights, density, near_pairs, gap_pairs):
    whole = pl.BlockSpec(memory_space=pltpu.VMEM)
    return pl.pallas_call(
        pack_kernel,
        out_shape=[jax.ShapeDtypeStruct((16, points.shape[2]), f32)] * 2,
        in_specs=[pl.BlockSpec(memory_space=pltpu.HBM)] * 5,
        out_specs=[whole] * 2,
        scratch_shapes=[pltpu.VMEM(x.shape, x.dtype) for x in (points, weights, density, near_pairs, gap_pairs)]
        + [pltpu.SemaphoreType.DMA((5,))],
        compiler_params=pltpu.CompilerParams(vmem_limit_bytes=8 * 1024 * 1024),
        name="pack",
    )(*[pltpu.with_memory_space_constraint(x, pltpu.HBM) for x in (points, weights, density, near_pairs, gap_pairs)])


near_partners = (
    lambda i: i ^ 1,
    lambda i: ((i + 1) ^ 1) - 1,
    lambda i: i ^ 2,
    lambda i: ((i + 2) ^ 2) - 2,
)


def swapped(block, axis, partner):
    size = lax.axis_size(axis)
    route = [(i, partner(i)) for i in range(size) if 0 <= partner(i) < size]
    return lax.ppermute(block, axis, route)


def per_device(points, weights, density, near_pairs, gap_pairs):
    sent, local = packed(points, weights, density, near_pairs, gap_pairs)
    tables = [local]
    for slot in TABLE_ORDER:
        if slot > 4:
            tables.append(swapped(sent, "section", lambda i, k=slot - 4: i ^ k))
        else:
            tables.append(swapped(sent, "dev", near_partners[slot - 1]))
    kept = pair_sums(tables[:1])
    return pair_sums(tables, kept)[0]


def solution(mesh):
    placed = (
        P(None, None, ("section", "dev")),
        P(None, ("section", "dev")),
        P(None, ("section", "dev")),
        P(None, ("section", "dev")),
        P(None, ("section", "dev")),
    )
    return jax.shard_map(
        per_device,
        mesh=mesh,
        in_specs=placed,
        out_specs=P(None, ("section", "dev")),
        check_vma=False,
    )
```

```python
import functools
import math

import jax
import jax.numpy as jnp
from jax import lax
from jax.experimental import pallas as pl
from jax.experimental.pallas import tpu as pltpu
from jax.sharding import PartitionSpec as P

CL = 128
QUAD = 3
DEPTH = 48
TURNED = 64
UNROLL = 12
TABLE_ORDER = (4, 3, 7, 5, 6, 2, 1)

smoothing = 0.02
green_scale = 0.25 / math.pi
f32 = jnp.float32
bf16 = jnp.bfloat16


def rounded(x, magic):
    return (x + magic) - magic


def row_ids(like):
    return lax.broadcasted_iota(jnp.int32, like.shape, 0)


def parts_of(tile, row_limit):
    rows = row_ids(tile)
    live = jnp.logical_and(lax.rem(rows, 4) < 3, rows < row_limit)
    x = jnp.where(live, tile, 0.0)
    high = rounded(x, 49152.0)
    rest = x - high
    mid = rounded(rest, 96.0)
    low = rounded(rest - mid, 0.1875)
    rest = mid + low
    sq_high = high * high
    sq_rest = rest * (high + high + rest)

    def row_sum(v):
        u = v + pltpu.roll(v, 7, 0)
        return u + pltpu.roll(u, 6, 0)

    return high, mid, low, row_sum(sq_high), row_sum(sq_rest)


def square_parts(sum_high, sum_rest):
    rows = row_ids(sum_high)
    upper = rows < 4
    v = jnp.where(upper, sum_high, sum_rest)
    one = rounded(v, jnp.where(upper, 196608.0, 768.0))
    rest = v - one
    two = rounded(rest, jnp.where(upper, 768.0, 3.0))
    three = rest - two
    place = lax.rem(rows, 4)
    return jnp.where(place == 0, one, jnp.where(place == 1, two, jnp.where(place == 2, three, 0.0)))


def point_features(tile0, tile1):
    h0, m0, l0, sh0, sr0 = parts_of(tile0, 8)
    h1, m1, l1, sh1, sr1 = parts_of(tile1, 3)

    def spread(v, row):
        return jnp.broadcast_to(v[row : row + 1], v.shape)

    turn = lambda v: pltpu.roll(v, 4, 0)
    return (
        (h0, m0, l0, turn(l0), spread(sh0, 0), spread(sr0, 0)),
        (turn(h0), turn(m0), turn(l0), l0, spread(sh0, 4), spread(sr0, 4)),
        (h1, m1, l1, turn(l1), spread(sh1, 0), spread(sr1, 0)),
    )


def right_features(tile0, tile1):
    rows = row_ids(tile0)
    out = []
    for high, mid, low, low_turned, sum_high, sum_rest in point_features(tile0, tile1):
        ones = jnp.where(rows < 6, 1.0, 0.0)
        g0 = jnp.where(rows < 3, high, jnp.where(rows < 6, ones, pltpu.roll(mid, 6, 0)))
        g1 = square_parts(sum_high, sum_rest + smoothing * smoothing)
        g1 = jnp.where(rows == 7, pltpu.roll(mid, 5, 0), g1)
        g4 = jnp.where(rows < 4, mid, low_turned)
        out.append(jnp.concatenate([g0, g1, g0, g0, g4, g4], 0).astype(bf16))
    return out


def left_features(tile0, tile1):
    rows = row_ids(tile0)
    out = []
    for high, mid, low, low_turned, sum_high, sum_rest in point_features(tile0, tile1):
        sq = square_parts(sum_high, sum_rest)
        sq_high = pltpu.roll(sq, 3, 0)
        sq_rest = pltpu.roll(sq, 7, 0)
        first = rows < 3
        mids = jnp.logical_and(rows >= 3, rows < 6)
        h2 = jnp.where(first, -2.0 * high, 0.0)
        m2 = jnp.where(first, -2.0 * mid, 0.0)
        l2 = jnp.where(first, -2.0 * low, 0.0)
        b0 = jnp.where(mids, sq_high, h2)
        b1 = jnp.where(lax.rem(rows, 4) < 3, 1.0, jnp.where(rows == 7, pltpu.roll(l2, 5, 0), 0.0))
        b3 = jnp.where(rows < 6, l2, pltpu.roll(l2, 6, 0))
        b2 = jnp.where(mids, sq_rest, m2)
        b4 = h2 + pltpu.roll(h2, 4, 0)
        b5 = m2 + pltpu.roll(m2, 4, 0)
        out.append(jnp.concatenate([b0, b1, b2, b3, b4, b5], 0))
    return out


def pair_codes(here, local, others, codes):
    def lists(table, row):
        return [table[row : row + 1, k * CL : (k + 1) * CL].astype(jnp.int32) for k in range(3)]

    low5 = lambda v: jnp.bitwise_and(v, 31)
    up5 = lambda v: lax.shift_right_logical(v, 5)

    def coded(valid, here, slot, there):
        return jnp.where(valid, low5(here) + (slot * 32 + low5(there)) * 256, -1)

    first, second, listed = lists(local, 14)
    me = jnp.broadcast_to(up5(first[:, 0:1]), first.shape)
    my_dev, dev = low5(me), low5(up5(second))
    slot = jnp.full(first.shape, 4, jnp.int32)
    slot = jnp.where(dev == jnp.bitwise_xor(my_dev, 2), 3, slot)
    slot = jnp.where(dev == jnp.bitwise_xor(my_dev + 1, 1) - 1, 2, slot)
    slot = jnp.where(dev == jnp.bitwise_xor(my_dev, 1), 1, slot)
    slot = jnp.where(dev == my_dev, 0, slot)
    inside = slot == 0
    if here:
        codes[0:1, :] = coded(jnp.logical_and(listed > 0, inside), first, 0, second)
        inside = jnp.logical_and(inside, first != second)
        codes[1:2, :] = coded(jnp.logical_and(listed > 0, inside), second, 0, first)
        return
    codes[0:1, :] = coded(jnp.logical_and(listed > 0, slot > 0), first, slot, second)
    for slot_in in range(1, 5):
        first, second, listed = lists(others[slot_in - 1], 14)
        valid = jnp.logical_and(listed > 0, up5(second) == me)
        codes[slot_in : slot_in + 1, :] = coded(valid, second, slot_in, first)
    first, second, listed = lists(local, 15)
    slot = 4 + jnp.bitwise_xor(up5(me), up5(up5(second)))
    row = coded(listed > 0, first, slot, second)
    lanes = lax.broadcasted_iota(jnp.int32, row.shape, 1)
    for slot_in in range(5, 8):
        first, second, listed = lists(others[slot_in - 1], 15)
        valid = jnp.logical_and(listed > 0, up5(second) == me)
        incoming = coded(valid, second, slot_in, first)
        row = jnp.where(lanes < 32 * (slot_in - 4), row, pltpu.roll(incoming, 32 * (slot_in - 4), 1))
    codes[5:6, :] = row


WIDE = 8


def pair_kernel(here, clusters, *refs):
    tables = refs[:1] if here else refs[:8]
    local = tables[0]
    refs = refs[len(tables) :]
    if not here:
        tables = [local] + [tables[1 + TABLE_ORDER.index(slot)] for slot in range(1, 8)]
    if here:
        left, wide_w, acc = refs[:3]
        refs = refs[3:]
    else:
        left, wide_w, _, out, acc = refs[:5]
        refs = refs[5:]
    codes, codes_smem, sem, todo, right, raw = refs
    used = tables if here else tables[1:]
    base = 0 if here else clusters

    pair_codes(here, local, tables[1:], codes)
    lists_copy = pltpu.make_async_copy(codes, codes_smem, sem)
    lists_copy.start()

    def prepare_left(n, carry):
        for u in range(WIDE):
            c = n * WIDE + u
            lanes = pl.ds(pl.multiple_of(c * CL, CL), CL)
            tile0, tile1 = local[0:8, lanes], local[8:16, lanes]
            weight_rows = (tile0[3:4], tile0[7:8], tile1[3:4])
            for q, block in enumerate(left_features(tile0, tile1)):
                weight = jnp.broadcast_to(weight_rows[q] * green_scale, (8, CL))
                block = jnp.concatenate([block, weight, jnp.zeros((TURNED - DEPTH - 8, CL), f32)], 0)
                turned = jnp.transpose(block)
                left[c, q * CL : (q + 1) * CL, 0:TURNED] = turned.astype(bf16)
                wide_w[c, q * CL : (q + 1) * CL, :] = jnp.broadcast_to(turned[:, DEPTH : DEPTH + 1], (CL, CL))
            acc[c] = jnp.zeros((CL, CL), f32)
        return carry

    if here:
        lax.fori_loop(0, clusters // WIDE, prepare_left, 0)
    lists_copy.wait()

    steps = clusters // WIDE
    rows_of_codes = 2 if here else 6
    count = 0
    for table in range(len(used)):

        def prepare_right(n, count):
            lanes = pl.ds(pl.multiple_of(n * (WIDE * CL), WIDE * CL), WIDE * CL)
            tile0, tile1 = used[table][0:8, lanes], used[table][8:16, lanes]
            blocks = right_features(tile0, tile1)
            for u in range(WIDE):
                place = table * clusters + n * WIDE + u
                cut = slice(u * CL, (u + 1) * CL)
                for q in range(QUAD):
                    right[place, :, q * CL : (q + 1) * CL] = blocks[q][:, cut]
                raw[place, 0:8, :] = tile0[:, cut]
                raw[place, 8:16, :] = tile1[:, cut]
            rows = range(2) if here else ([table] if table < 6 else [])
            for row in rows:
                for u in range(CL // steps):
                    code = codes_smem[row, n * (CL // steps) + u]
                    todo[count] = code
                    count = count + (code >= 0).astype(jnp.int32)
            return count

        count = lax.fori_loop(0, steps, prepare_right, count)
    for extra in range(UNROLL - 1):
        todo[count + extra] = clusters + base * 256

    def tile_of(i, j):
        weight_b = (raw[j, 3:4, :], raw[j, 7:8, :], raw[j, 11:12, :])
        far = right[j]
        total = None
        for p in range(QUAD):
            near = left[i, p * CL : (p + 1) * CL, 0:DEPTH]
            dist = jnp.dot(near, far, preferred_element_type=f32)
            row = None
            for q in range(QUAD):
                term = weight_b[q] * lax.rsqrt(dist[:, q * CL : (q + 1) * CL])
                row = term if row is None else row + term
            row = row * wide_w[i, p * CL : (p + 1) * CL, :]
            total = row if total is None else total + row
        return total

    lower = lax.broadcasted_iota(jnp.int32, (1, CL), 1) < CL // 2

    def group(g, carry):
        done = []
        for u in range(UNROLL):
            code = todo[g * UNROLL + u]
            i = jnp.bitwise_and(code, 255)
            j = lax.shift_right_logical(code, 8) - base
            done.append((i, j, tile_of(i, j)))
        for i, j, tile in done:
            dens0, dens1 = raw[j, 12:13, :], raw[j, 13:14, :]
            same = tile * jnp.where(lower, dens0, dens1)
            other = tile * jnp.where(lower, dens1, dens0)
            acc[i] += same + pltpu.roll(other, CL // 2, 1)
        return carry

    lax.fori_loop(0, lax.div(count + UNROLL - 1, UNROLL), group, 0)

    if here:
        return

    rows = lax.broadcasted_iota(jnp.int32, (8, 2 * CL), 0)
    lanes_of = jnp.bitwise_and(lax.broadcasted_iota(jnp.int32, (8, 2 * CL), 1), CL - 1)
    chosen = jnp.where(rows == lanes_of // (CL // 2), 1.0, 0.0).astype(bf16)

    def finish(n, carry):
        for u in range(8):
            c = n * 8 + u
            lanes = pl.ds(pl.multiple_of(c * CL, CL), CL)
            value = acc[c]
            high = value.astype(bf16)
            low = (value - high.astype(f32)).astype(bf16)
            both = jnp.concatenate([high, low], 1)
            sums = lax.dot_general(chosen, both, (((1,), (1,)), ((), ())), preferred_element_type=f32)
            out[:, lanes] = sums[0:2]
        return carry

    lax.fori_loop(0, clusters // 8, finish, 0)


def pair_sums(tables, kept=None):
    here = kept is None
    panels = tables[0].shape[1]
    clusters = panels // CL
    places = (1 if here else len(tables) - 1) * clusters
    whole = pl.BlockSpec(memory_space=pltpu.VMEM)
    result = jax.ShapeDtypeStruct((2, panels), f32)
    left = jax.ShapeDtypeStruct((clusters + 1, QUAD * CL, CL), bf16)
    wide = jax.ShapeDtypeStruct((clusters + 1, QUAD * CL, CL), f32)
    acc = jax.ShapeDtypeStruct((clusters + 1, CL, CL), f32)
    return pl.pallas_call(
        functools.partial(pair_kernel, here, clusters),
        out_shape=[left, wide, acc] if here else [result, acc],
        in_specs=[whole] * (len(tables) + (0 if here else 3)),
        out_specs=[whole] * (3 if here else 2),
        input_output_aliases={} if here else {len(tables) + 2: 1},
        scratch_shapes=[
            pltpu.VMEM((8, CL), jnp.int32),
            pltpu.SMEM((8, CL), jnp.int32),
            pltpu.SemaphoreType.DMA,
            pltpu.SMEM((8 * CL + UNROLL,), jnp.int32),
            pltpu.VMEM((places, DEPTH, QUAD * CL), bf16),
            pltpu.VMEM((places, 16, CL), f32),
        ],
        compiler_params=pltpu.CompilerParams(vmem_limit_bytes=32 * 1024 * 1024),
        cost_estimate=pl.CostEstimate(
            flops=2_000_000_000, bytes_accessed=(40 if here else 80) * 1024 * 1024, transcendentals=10_000_000
        ),
        name="pairs_here" if here else "pairs_across",
    )(*tables, *(kept or ()))


def pack_kernel(*refs):
    sent, out = refs[5:7]
    points, weights, density, near_pairs, gap_pairs = refs[7:12]
    copies = [pltpu.make_async_copy(refs[k], refs[7 + k], refs[12].at[k]) for k in range(5)]
    for copy in copies:
        copy.start()
    for copy in copies:
        copy.wait()
    for q in range(QUAD):
        for c in range(3):
            out[4 * q + c : 4 * q + c + 1, :] = points[c, q : q + 1, :]
        out[4 * q + 3 : 4 * q + 4, :] = weights[q : q + 1, :]
    out[12:14, :] = density[...]
    out[14:16, :] = jnp.zeros((2, out.shape[1]), f32)
    for k in range(3):
        out[14:15, k * CL : k * CL + near_pairs.shape[1]] = near_pairs[k : k + 1, :].astype(f32)
        out[15:16, k * CL : k * CL + gap_pairs.shape[1]] = gap_pairs[k : k + 1, :].astype(f32)
    sent[...] = out[...]


def packed(points, weights, density, near_pairs, gap_pairs):
    whole = pl.BlockSpec(memory_space=pltpu.VMEM)
    return pl.pallas_call(
        pack_kernel,
        out_shape=[jax.ShapeDtypeStruct((16, points.shape[2]), f32)] * 2,
        in_specs=[pl.BlockSpec(memory_space=pltpu.HBM)] * 5,
        out_specs=[whole] * 2,
        scratch_shapes=[pltpu.VMEM(x.shape, x.dtype) for x in (points, weights, density, near_pairs, gap_pairs)]
        + [pltpu.SemaphoreType.DMA((5,))],
        compiler_params=pltpu.CompilerParams(vmem_limit_bytes=8 * 1024 * 1024),
        name="pack",
    )(*[pltpu.with_memory_space_constraint(x, pltpu.HBM) for x in (points, weights, density, near_pairs, gap_pairs)])


near_partners = (
    lambda i: i ^ 1,
    lambda i: ((i + 1) ^ 1) - 1,
    lambda i: i ^ 2,
    lambda i: ((i + 2) ^ 2) - 2,
)


def swapped(block, axis, partner):
    size = lax.axis_size(axis)
    route = [(i, partner(i)) for i in range(size) if 0 <= partner(i) < size]
    return lax.ppermute(block, axis, route)


def per_device(points, weights, density, near_pairs, gap_pairs):
    sent, local = packed(points, weights, density, near_pairs, gap_pairs)
    tables = [local]
    for slot in TABLE_ORDER:
        if slot > 4:
            tables.append(swapped(sent, "section", lambda i, k=slot - 4: i ^ k))
        else:
            tables.append(swapped(sent, "dev", near_partners[slot - 1]))
    kept = pair_sums(tables[:1])
    return pair_sums(tables, kept)[0]


def solution(mesh):
    placed = (
        P(None, None, ("section", "dev")),
        P(None, ("section", "dev")),
        P(None, ("section", "dev")),
        P(None, ("section", "dev")),
        P(None, ("section", "dev")),
    )
    return jax.shard_map(
        per_device,
        mesh=mesh,
        in_specs=placed,
        out_specs=P(None, ("section", "dev")),
        check_vma=False,
    )
```

```python
import functools
import math

import jax
import jax.numpy as jnp
from jax import lax
from jax.experimental import pallas as pl
from jax.experimental.pallas import tpu as pltpu
from jax.sharding import PartitionSpec as P

CL = 128
QUAD = 3
DEPTH = 48
TURNED = 64
UNROLL = 12
TABLE_ORDER = (3, 7, 4, 5, 6, 2, 1)

smoothing = 0.02
green_scale = 0.25 / math.pi
f32 = jnp.float32
bf16 = jnp.bfloat16


def rounded(x, magic):
    return (x + magic) - magic


def row_ids(like):
    return lax.broadcasted_iota(jnp.int32, like.shape, 0)


def parts_of(tile, row_limit):
    rows = row_ids(tile)
    live = jnp.logical_and(lax.rem(rows, 4) < 3, rows < row_limit)
    x = jnp.where(live, tile, 0.0)
    high = rounded(x, 49152.0)
    rest = x - high
    mid = rounded(rest, 96.0)
    low = rounded(rest - mid, 0.1875)
    rest = mid + low
    sq_high = high * high
    sq_rest = rest * (high + high + rest)

    def row_sum(v):
        u = v + pltpu.roll(v, 7, 0)
        return u + pltpu.roll(u, 6, 0)

    return high, mid, low, row_sum(sq_high), row_sum(sq_rest)


def square_parts(sum_high, sum_rest):
    rows = row_ids(sum_high)
    upper = rows < 4
    v = jnp.where(upper, sum_high, sum_rest)
    one = rounded(v, jnp.where(upper, 196608.0, 768.0))
    rest = v - one
    two = rounded(rest, jnp.where(upper, 768.0, 3.0))
    three = rest - two
    place = lax.rem(rows, 4)
    return jnp.where(place == 0, one, jnp.where(place == 1, two, jnp.where(place == 2, three, 0.0)))


def point_features(tile0, tile1):
    h0, m0, l0, sh0, sr0 = parts_of(tile0, 8)
    h1, m1, l1, sh1, sr1 = parts_of(tile1, 3)

    def spread(v, row):
        return jnp.broadcast_to(v[row : row + 1], v.shape)

    turn = lambda v: pltpu.roll(v, 4, 0)
    return (
        (h0, m0, l0, turn(l0), spread(sh0, 0), spread(sr0, 0)),
        (turn(h0), turn(m0), turn(l0), l0, spread(sh0, 4), spread(sr0, 4)),
        (h1, m1, l1, turn(l1), spread(sh1, 0), spread(sr1, 0)),
    )


def right_features(tile0, tile1):
    rows = row_ids(tile0)
    out = []
    for high, mid, low, low_turned, sum_high, sum_rest in point_features(tile0, tile1):
        ones = jnp.where(rows < 6, 1.0, 0.0)
        g0 = jnp.where(rows < 3, high, jnp.where(rows < 6, ones, pltpu.roll(mid, 6, 0)))
        g1 = square_parts(sum_high, sum_rest + smoothing * smoothing)
        g1 = jnp.where(rows == 7, pltpu.roll(mid, 5, 0), g1)
        g4 = jnp.where(rows < 4, mid, low_turned)
        out.append(jnp.concatenate([g0, g1, g0, g0, g4, g4], 0).astype(bf16))
    return out


def left_features(tile0, tile1):
    rows = row_ids(tile0)
    out = []
    for high, mid, low, low_turned, sum_high, sum_rest in point_features(tile0, tile1):
        sq = square_parts(sum_high, sum_rest)
        sq_high = pltpu.roll(sq, 3, 0)
        sq_rest = pltpu.roll(sq, 7, 0)
        first = rows < 3
        mids = jnp.logical_and(rows >= 3, rows < 6)
        h2 = jnp.where(first, -2.0 * high, 0.0)
        m2 = jnp.where(first, -2.0 * mid, 0.0)
        l2 = jnp.where(first, -2.0 * low, 0.0)
        b0 = jnp.where(mids, sq_high, h2)
        b1 = jnp.where(lax.rem(rows, 4) < 3, 1.0, jnp.where(rows == 7, pltpu.roll(l2, 5, 0), 0.0))
        b3 = jnp.where(rows < 6, l2, pltpu.roll(l2, 6, 0))
        b2 = jnp.where(mids, sq_rest, m2)
        b4 = h2 + pltpu.roll(h2, 4, 0)
        b5 = m2 + pltpu.roll(m2, 4, 0)
        out.append(jnp.concatenate([b0, b1, b2, b3, b4, b5], 0))
    return out


def pair_codes(here, local, others, codes):
    def lists(table, row):
        return [table[row : row + 1, k * CL : (k + 1) * CL].astype(jnp.int32) for k in range(3)]

    low5 = lambda v: jnp.bitwise_and(v, 31)
    up5 = lambda v: lax.shift_right_logical(v, 5)

    def coded(valid, here, slot, there):
        return jnp.where(valid, low5(here) + (slot * 32 + low5(there)) * 256, -1)

    first, second, listed = lists(local, 14)
    me = jnp.broadcast_to(up5(first[:, 0:1]), first.shape)
    my_dev, dev = low5(me), low5(up5(second))
    slot = jnp.full(first.shape, 4, jnp.int32)
    slot = jnp.where(dev == jnp.bitwise_xor(my_dev, 2), 3, slot)
    slot = jnp.where(dev == jnp.bitwise_xor(my_dev + 1, 1) - 1, 2, slot)
    slot = jnp.where(dev == jnp.bitwise_xor(my_dev, 1), 1, slot)
    slot = jnp.where(dev == my_dev, 0, slot)
    inside = slot == 0
    if here:
        codes[0:1, :] = coded(jnp.logical_and(listed > 0, inside), first, 0, second)
        inside = jnp.logical_and(inside, first != second)
        codes[1:2, :] = coded(jnp.logical_and(listed > 0, inside), second, 0, first)
        return
    codes[0:1, :] = coded(jnp.logical_and(listed > 0, slot > 0), first, slot, second)
    for slot_in in range(1, 5):
        first, second, listed = lists(others[slot_in - 1], 14)
        valid = jnp.logical_and(listed > 0, up5(second) == me)
        codes[slot_in : slot_in + 1, :] = coded(valid, second, slot_in, first)
    first, second, listed = lists(local, 15)
    slot = 4 + jnp.bitwise_xor(up5(me), up5(up5(second)))
    row = coded(listed > 0, first, slot, second)
    lanes = lax.broadcasted_iota(jnp.int32, row.shape, 1)
    for slot_in in range(5, 8):
        first, second, listed = lists(others[slot_in - 1], 15)
        valid = jnp.logical_and(listed > 0, up5(second) == me)
        incoming = coded(valid, second, slot_in, first)
        row = jnp.where(lanes < 32 * (slot_in - 4), row, pltpu.roll(incoming, 32 * (slot_in - 4), 1))
    codes[5:6, :] = row


WIDE = 8


def pair_kernel(here, clusters, *refs):
    tables = refs[:1] if here else refs[:8]
    local = tables[0]
    refs = refs[len(tables) :]
    if not here:
        tables = [local] + [tables[1 + TABLE_ORDER.index(slot)] for slot in range(1, 8)]
    if here:
        left, wide_w, acc = refs[:3]
        refs = refs[3:]
    else:
        left, wide_w, _, out, acc = refs[:5]
        refs = refs[5:]
    codes, codes_smem, sem, todo, right, raw = refs
    used = tables if here else tables[1:]
    base = 0 if here else clusters

    pair_codes(here, local, tables[1:], codes)
    lists_copy = pltpu.make_async_copy(codes, codes_smem, sem)
    lists_copy.start()

    def prepare_left(n, carry):
        for u in range(WIDE):
            c = n * WIDE + u
            lanes = pl.ds(pl.multiple_of(c * CL, CL), CL)
            tile0, tile1 = local[0:8, lanes], local[8:16, lanes]
            weight_rows = (tile0[3:4], tile0[7:8], tile1[3:4])
            for q, block in enumerate(left_features(tile0, tile1)):
                weight = jnp.broadcast_to(weight_rows[q] * green_scale, (8, CL))
                block = jnp.concatenate([block, weight, jnp.zeros((TURNED - DEPTH - 8, CL), f32)], 0)
                turned = jnp.transpose(block)
                left[c, q * CL : (q + 1) * CL, 0:TURNED] = turned.astype(bf16)
                wide_w[c, q * CL : (q + 1) * CL, :] = jnp.broadcast_to(turned[:, DEPTH : DEPTH + 1], (CL, CL))
            acc[c] = jnp.zeros((CL, CL), f32)
        return carry

    if here:
        lax.fori_loop(0, clusters // WIDE, prepare_left, 0)
    lists_copy.wait()

    steps = clusters // WIDE
    rows_of_codes = 2 if here else 6
    count = 0
    for table in range(len(used)):

        def prepare_right(n, count):
            lanes = pl.ds(pl.multiple_of(n * (WIDE * CL), WIDE * CL), WIDE * CL)
            tile0, tile1 = used[table][0:8, lanes], used[table][8:16, lanes]
            blocks = right_features(tile0, tile1)
            for u in range(WIDE):
                place = table * clusters + n * WIDE + u
                cut = slice(u * CL, (u + 1) * CL)
                for q in range(QUAD):
                    right[place, :, q * CL : (q + 1) * CL] = blocks[q][:, cut]
                raw[place, 0:8, :] = tile0[:, cut]
                raw[place, 8:16, :] = tile1[:, cut]
            rows = range(2) if here else ([table] if table < 6 else [])
            for row in rows:
                for u in range(CL // steps):
                    code = codes_smem[row, n * (CL // steps) + u]
                    todo[count] = code
                    count = count + (code >= 0).astype(jnp.int32)
            return count

        count = lax.fori_loop(0, steps, prepare_right, count)
    for extra in range(UNROLL - 1):
        todo[count + extra] = clusters + base * 256

    def tile_of(i, j):
        weight_b = (raw[j, 3:4, :], raw[j, 7:8, :], raw[j, 11:12, :])
        far = right[j]
        total = None
        for p in range(QUAD):
            near = left[i, p * CL : (p + 1) * CL, 0:DEPTH]
            dist = jnp.dot(near, far, preferred_element_type=f32)
            row = None
            for q in range(QUAD):
                term = weight_b[q] * lax.rsqrt(dist[:, q * CL : (q + 1) * CL])
                row = term if row is None else row + term
            row = row * wide_w[i, p * CL : (p + 1) * CL, :]
            total = row if total is None else total + row
        return total

    lower = lax.broadcasted_iota(jnp.int32, (1, CL), 1) < CL // 2

    def group(g, carry):
        done = []
        for u in range(UNROLL):
            code = todo[g * UNROLL + u]
            i = jnp.bitwise_and(code, 255)
            j = lax.shift_right_logical(code, 8) - base
            done.append((i, j, tile_of(i, j)))
        for i, j, tile in done:
            dens0, dens1 = raw[j, 12:13, :], raw[j, 13:14, :]
            same = tile * jnp.where(lower, dens0, dens1)
            other = tile * jnp.where(lower, dens1, dens0)
            acc[i] += same + pltpu.roll(other, CL // 2, 1)
        return carry

    lax.fori_loop(0, lax.div(count + UNROLL - 1, UNROLL), group, 0)

    if here:
        return

    rows = lax.broadcasted_iota(jnp.int32, (8, 2 * CL), 0)
    lanes_of = jnp.bitwise_and(lax.broadcasted_iota(jnp.int32, (8, 2 * CL), 1), CL - 1)
    chosen = jnp.where(rows == lanes_of // (CL // 2), 1.0, 0.0).astype(bf16)

    def finish(n, carry):
        for u in range(8):
            c = n * 8 + u
            lanes = pl.ds(pl.multiple_of(c * CL, CL), CL)
            value = acc[c]
            high = value.astype(bf16)
            low = (value - high.astype(f32)).astype(bf16)
            both = jnp.concatenate([high, low], 1)
            sums = lax.dot_general(chosen, both, (((1,), (1,)), ((), ())), preferred_element_type=f32)
            out[:, lanes] = sums[0:2]
        return carry

    lax.fori_loop(0, clusters // 8, finish, 0)


def pair_sums(tables, kept=None):
    here = kept is None
    panels = tables[0].shape[1]
    clusters = panels // CL
    places = (1 if here else len(tables) - 1) * clusters
    whole = pl.BlockSpec(memory_space=pltpu.VMEM)
    result = jax.ShapeDtypeStruct((2, panels), f32)
    left = jax.ShapeDtypeStruct((clusters + 1, QUAD * CL, CL), bf16)
    wide = jax.ShapeDtypeStruct((clusters + 1, QUAD * CL, CL), f32)
    acc = jax.ShapeDtypeStruct((clusters + 1, CL, CL), f32)
    return pl.pallas_call(
        functools.partial(pair_kernel, here, clusters),
        out_shape=[left, wide, acc] if here else [result, acc],
        in_specs=[whole] * (len(tables) + (0 if here else 3)),
        out_specs=[whole] * (3 if here else 2),
        input_output_aliases={} if here else {len(tables) + 2: 1},
        scratch_shapes=[
            pltpu.VMEM((8, CL), jnp.int32),
            pltpu.SMEM((8, CL), jnp.int32),
            pltpu.SemaphoreType.DMA,
            pltpu.SMEM((8 * CL + UNROLL,), jnp.int32),
            pltpu.VMEM((places, DEPTH, QUAD * CL), bf16),
            pltpu.VMEM((places, 16, CL), f32),
        ],
        compiler_params=pltpu.CompilerParams(vmem_limit_bytes=32 * 1024 * 1024),
        cost_estimate=pl.CostEstimate(
            flops=2_000_000_000, bytes_accessed=(40 if here else 80) * 1024 * 1024, transcendentals=10_000_000
        ),
        name="pairs_here" if here else "pairs_across",
    )(*tables, *(kept or ()))


def pack_kernel(*refs):
    sent, out = refs[5:7]
    points, weights, density, near_pairs, gap_pairs = refs[7:12]
    copies = [pltpu.make_async_copy(refs[k], refs[7 + k], refs[12].at[k]) for k in range(5)]
    for copy in copies:
        copy.start()
    for copy in copies:
        copy.wait()
    for q in range(QUAD):
        for c in range(3):
            out[4 * q + c : 4 * q + c + 1, :] = points[c, q : q + 1, :]
        out[4 * q + 3 : 4 * q + 4, :] = weights[q : q + 1, :]
    out[12:14, :] = density[...]
    out[14:16, :] = jnp.zeros((2, out.shape[1]), f32)
    for k in range(3):
        out[14:15, k * CL : k * CL + near_pairs.shape[1]] = near_pairs[k : k + 1, :].astype(f32)
        out[15:16, k * CL : k * CL + gap_pairs.shape[1]] = gap_pairs[k : k + 1, :].astype(f32)
    sent[...] = out[...]


def packed(points, weights, density, near_pairs, gap_pairs):
    whole = pl.BlockSpec(memory_space=pltpu.VMEM)
    return pl.pallas_call(
        pack_kernel,
        out_shape=[jax.ShapeDtypeStruct((16, points.shape[2]), f32)] * 2,
        in_specs=[pl.BlockSpec(memory_space=pltpu.HBM)] * 5,
        out_specs=[whole] * 2,
        scratch_shapes=[pltpu.VMEM(x.shape, x.dtype) for x in (points, weights, density, near_pairs, gap_pairs)]
        + [pltpu.SemaphoreType.DMA((5,))],
        compiler_params=pltpu.CompilerParams(vmem_limit_bytes=8 * 1024 * 1024),
        name="pack",
    )(*[pltpu.with_memory_space_constraint(x, pltpu.HBM) for x in (points, weights, density, near_pairs, gap_pairs)])


near_partners = (
    lambda i: i ^ 1,
    lambda i: ((i + 1) ^ 1) - 1,
    lambda i: i ^ 2,
    lambda i: ((i + 2) ^ 2) - 2,
)


def swapped(block, axis, partner):
    size = lax.axis_size(axis)
    route = [(i, partner(i)) for i in range(size) if 0 <= partner(i) < size]
    return lax.ppermute(block, axis, route)


def per_device(points, weights, density, near_pairs, gap_pairs):
    sent, local = packed(points, weights, density, near_pairs, gap_pairs)
    tables = [local]
    for slot in TABLE_ORDER:
        if slot > 4:
            tables.append(swapped(sent, "section", lambda i, k=slot - 4: i ^ k))
        else:
            tables.append(swapped(sent, "dev", near_partners[slot - 1]))
    kept = pair_sums(tables[:1])
    return pair_sums(tables, kept)[0]


def solution(mesh):
    placed = (
        P(None, None, ("section", "dev")),
        P(None, ("section", "dev")),
        P(None, ("section", "dev")),
        P(None, ("section", "dev")),
        P(None, ("section", "dev")),
    )
    return jax.shard_map(
        per_device,
        mesh=mesh,
        in_specs=placed,
        out_specs=P(None, ("section", "dev")),
        check_vma=False,
    )
```

```python
import functools
import math

import jax
import jax.numpy as jnp
from jax import lax
from jax.experimental import pallas as pl
from jax.experimental.pallas import tpu as pltpu
from jax.sharding import PartitionSpec as P

CL = 128
QUAD = 3
DEPTH = 48
TURNED = 64
UNROLL = 14
TABLE_ORDER = (3, 7, 4, 5, 6, 2, 1)

smoothing = 0.02
green_scale = 0.25 / math.pi
f32 = jnp.float32
bf16 = jnp.bfloat16


def rounded(x, magic):
    return (x + magic) - magic


def row_ids(like):
    return lax.broadcasted_iota(jnp.int32, like.shape, 0)


def parts_of(tile, row_limit):
    rows = row_ids(tile)
    live = jnp.logical_and(jnp.bitwise_and(rows, 3) < 3, rows < row_limit)
    x = jnp.where(live, tile, 0.0)
    high = rounded(x, 49152.0)
    rest = x - high
    mid = rounded(rest, 96.0)
    low = rounded(rest - mid, 0.1875)
    rest = mid + low
    sq_high = high * high
    sq_rest = rest * (high + high + rest)

    def row_sum(v):
        u = v + pltpu.roll(v, 7, 0)
        return u + pltpu.roll(u, 6, 0)

    return high, mid, low, row_sum(sq_high), row_sum(sq_rest)


def square_parts(sum_high, sum_rest):
    rows = row_ids(sum_high)
    upper = rows < 4
    v = jnp.where(upper, sum_high, sum_rest)
    one = rounded(v, jnp.where(upper, 196608.0, 768.0))
    rest = v - one
    two = rounded(rest, jnp.where(upper, 768.0, 3.0))
    three = rest - two
    place = jnp.bitwise_and(rows, 3)
    return jnp.where(place == 0, one, jnp.where(place == 1, two, jnp.where(place == 2, three, 0.0)))


def point_features(tile0, tile1):
    h0, m0, l0, sh0, sr0 = parts_of(tile0, 8)
    h1, m1, l1, sh1, sr1 = parts_of(tile1, 3)

    def spread(v, row):
        return jnp.broadcast_to(v[row : row + 1], v.shape)

    turn = lambda v: pltpu.roll(v, 4, 0)
    return (
        (h0, m0, l0, turn(l0), spread(sh0, 0), spread(sr0, 0)),
        (turn(h0), turn(m0), turn(l0), l0, spread(sh0, 4), spread(sr0, 4)),
        (h1, m1, l1, turn(l1), spread(sh1, 0), spread(sr1, 0)),
    )


def right_features(tile0, tile1):
    rows = row_ids(tile0)
    out = []
    for high, mid, low, low_turned, sum_high, sum_rest in point_features(tile0, tile1):
        ones = jnp.where(rows < 6, 1.0, 0.0)
        g0 = jnp.where(rows < 3, high, jnp.where(rows < 6, ones, pltpu.roll(mid, 6, 0)))
        g1 = square_parts(sum_high, sum_rest + smoothing * smoothing)
        g1 = jnp.where(rows == 7, pltpu.roll(mid, 5, 0), g1)
        g4 = jnp.where(rows < 4, mid, low_turned)
        out.append(jnp.concatenate([g0, g1, g0, g0, g4, g4], 0).astype(bf16))
    return out


def left_features(tile0, tile1):
    rows = row_ids(tile0)
    out = []
    for high, mid, low, low_turned, sum_high, sum_rest in point_features(tile0, tile1):
        sq = square_parts(sum_high, sum_rest)
        sq_high = pltpu.roll(sq, 3, 0)
        sq_rest = pltpu.roll(sq, 7, 0)
        first = rows < 3
        mids = jnp.logical_and(rows >= 3, rows < 6)
        h2 = jnp.where(first, -2.0 * high, 0.0)
        m2 = jnp.where(first, -2.0 * mid, 0.0)
        l2 = jnp.where(first, -2.0 * low, 0.0)
        b0 = jnp.where(mids, sq_high, h2)
        b1 = jnp.where(jnp.bitwise_and(rows, 3) < 3, 1.0, jnp.where(rows == 7, pltpu.roll(l2, 5, 0), 0.0))
        b3 = jnp.where(rows < 6, l2, pltpu.roll(l2, 6, 0))
        b2 = jnp.where(mids, sq_rest, m2)
        b4 = h2 + pltpu.roll(h2, 4, 0)
        b5 = m2 + pltpu.roll(m2, 4, 0)
        out.append(jnp.concatenate([b0, b1, b2, b3, b4, b5], 0))
    return out


def pair_codes(here, local, others, codes):
    def lists(table, row):
        return [table[row : row + 1, k * CL : (k + 1) * CL].astype(jnp.int32) for k in range(3)]

    low5 = lambda v: jnp.bitwise_and(v, 31)
    up5 = lambda v: lax.shift_right_logical(v, 5)

    def coded(valid, here, slot, there):
        return jnp.where(valid, low5(here) + (slot * 32 + low5(there)) * 256, -1)

    first, second, listed = lists(local, 14)
    me = jnp.broadcast_to(up5(first[:, 0:1]), first.shape)
    my_dev, dev = low5(me), low5(up5(second))
    slot = jnp.full(first.shape, 4, jnp.int32)
    slot = jnp.where(dev == jnp.bitwise_xor(my_dev, 2), 3, slot)
    slot = jnp.where(dev == jnp.bitwise_xor(my_dev + 1, 1) - 1, 2, slot)
    slot = jnp.where(dev == jnp.bitwise_xor(my_dev, 1), 1, slot)
    slot = jnp.where(dev == my_dev, 0, slot)
    inside = slot == 0
    if here:
        codes[0:1, :] = coded(jnp.logical_and(listed > 0, inside), first, 0, second)
        inside = jnp.logical_and(inside, first != second)
        codes[1:2, :] = coded(jnp.logical_and(listed > 0, inside), second, 0, first)
        return
    codes[0:1, :] = coded(jnp.logical_and(listed > 0, slot > 0), first, slot, second)
    for slot_in in range(1, 5):
        first, second, listed = lists(others[slot_in - 1], 14)
        valid = jnp.logical_and(listed > 0, up5(second) == me)
        codes[slot_in : slot_in + 1, :] = coded(valid, second, slot_in, first)
    first, second, listed = lists(local, 15)
    slot = 4 + jnp.bitwise_xor(up5(me), up5(up5(second)))
    row = coded(listed > 0, first, slot, second)
    lanes = lax.broadcasted_iota(jnp.int32, row.shape, 1)
    for slot_in in range(5, 8):
        first, second, listed = lists(others[slot_in - 1], 15)
        valid = jnp.logical_and(listed > 0, up5(second) == me)
        incoming = coded(valid, second, slot_in, first)
        row = jnp.where(lanes < 32 * (slot_in - 4), row, pltpu.roll(incoming, 32 * (slot_in - 4), 1))
    codes[5:6, :] = row


WIDE = 8


def pair_kernel(here, clusters, *refs):
    tables = refs[:1] if here else refs[:8]
    local = tables[0]
    refs = refs[len(tables) :]
    if not here:
        tables = [local] + [tables[1 + TABLE_ORDER.index(slot)] for slot in range(1, 8)]
    if here:
        left, wide_w, acc = refs[:3]
        refs = refs[3:]
    else:
        left, wide_w, _, out, acc = refs[:5]
        refs = refs[5:]
    codes, codes_smem, sem, todo, right, raw = refs
    used = tables if here else tables[1:]
    base = 0 if here else clusters

    pair_codes(here, local, tables[1:], codes)
    lists_copy = pltpu.make_async_copy(codes, codes_smem, sem)
    lists_copy.start()

    def prepare_left(n, carry):
        for u in range(WIDE):
            c = n * WIDE + u
            lanes = pl.ds(pl.multiple_of(c * CL, CL), CL)
            tile0, tile1 = local[0:8, lanes], local[8:16, lanes]
            weight_rows = (tile0[3:4], tile0[7:8], tile1[3:4])
            for q, block in enumerate(left_features(tile0, tile1)):
                weight = jnp.broadcast_to(weight_rows[q] * green_scale, (8, CL))
                block = jnp.concatenate([block, weight, jnp.zeros((TURNED - DEPTH - 8, CL), f32)], 0)
                turned = jnp.transpose(block)
                left[c, q * CL : (q + 1) * CL, 0:TURNED] = turned.astype(bf16)
                wide_w[c, q * CL : (q + 1) * CL, :] = jnp.broadcast_to(turned[:, DEPTH : DEPTH + 1], (CL, CL))
            acc[c] = jnp.zeros((CL, CL), f32)
        return carry

    if here:
        lax.fori_loop(0, clusters // WIDE, prepare_left, 0)
    lists_copy.wait()

    steps = clusters // WIDE
    rows_of_codes = 2 if here else 6
    count = 0
    for table in range(len(used)):

        def prepare_right(n, count):
            lanes = pl.ds(pl.multiple_of(n * (WIDE * CL), WIDE * CL), WIDE * CL)
            tile0, tile1 = used[table][0:8, lanes], used[table][8:16, lanes]
            blocks = right_features(tile0, tile1)
            for u in range(WIDE):
                place = table * clusters + n * WIDE + u
                cut = slice(u * CL, (u + 1) * CL)
                for q in range(QUAD):
                    right[place, :, q * CL : (q + 1) * CL] = blocks[q][:, cut]
                raw[place, 0:8, :] = tile0[:, cut]
                raw[place, 8:16, :] = tile1[:, cut]
            rows = range(2) if here else ([table] if table < 6 else [])
            for row in rows:
                for u in range(CL // steps):
                    code = codes_smem[row, n * (CL // steps) + u]
                    todo[count] = code
                    count = count + (code >= 0).astype(jnp.int32)
            return count

        count = lax.fori_loop(0, steps, prepare_right, count)
    for extra in range(UNROLL - 1):
        todo[count + extra] = clusters + base * 256

    def tile_of(i, j):
        weight_b = (raw[j, 3:4, :], raw[j, 7:8, :], raw[j, 11:12, :])
        far = right[j]
        total = None
        for p in range(QUAD):
            near = left[i, p * CL : (p + 1) * CL, 0:DEPTH]
            dist = jnp.dot(near, far, preferred_element_type=f32)
            row = None
            for q in range(QUAD):
                term = weight_b[q] * lax.rsqrt(dist[:, q * CL : (q + 1) * CL])
                row = term if row is None else row + term
            row = row * wide_w[i, p * CL : (p + 1) * CL, :]
            total = row if total is None else total + row
        return total

    lower = lax.broadcasted_iota(jnp.int32, (1, CL), 1) < CL // 2

    def group(g, carry):
        done = []
        for u in range(UNROLL):
            code = todo[g * UNROLL + u]
            i = jnp.bitwise_and(code, 255)
            j = lax.shift_right_logical(code, 8) - base
            done.append((i, j, tile_of(i, j)))
        for i, j, tile in done:
            dens0, dens1 = raw[j, 12:13, :], raw[j, 13:14, :]
            same = tile * jnp.where(lower, dens0, dens1)
            other = tile * jnp.where(lower, dens1, dens0)
            acc[i] += same + pltpu.roll(other, CL // 2, 1)
        return carry

    lax.fori_loop(0, lax.div(count + UNROLL - 1, UNROLL), group, 0)

    if here:
        return

    rows = lax.broadcasted_iota(jnp.int32, (8, 2 * CL), 0)
    lanes_of = jnp.bitwise_and(lax.broadcasted_iota(jnp.int32, (8, 2 * CL), 1), CL - 1)
    chosen = jnp.where(rows == lanes_of // (CL // 2), 1.0, 0.0).astype(bf16)

    def finish(n, carry):
        for u in range(8):
            c = n * 8 + u
            lanes = pl.ds(pl.multiple_of(c * CL, CL), CL)
            value = acc[c]
            high = value.astype(bf16)
            low = (value - high.astype(f32)).astype(bf16)
            both = jnp.concatenate([high, low], 1)
            sums = lax.dot_general(chosen, both, (((1,), (1,)), ((), ())), preferred_element_type=f32)
            out[:, lanes] = sums[0:2]
        return carry

    lax.fori_loop(0, clusters // 8, finish, 0)


def pair_sums(tables, kept=None):
    here = kept is None
    panels = tables[0].shape[1]
    clusters = panels // CL
    places = (1 if here else len(tables) - 1) * clusters
    whole = pl.BlockSpec(memory_space=pltpu.VMEM)
    result = jax.ShapeDtypeStruct((2, panels), f32)
    left = jax.ShapeDtypeStruct((clusters + 1, QUAD * CL, CL), bf16)
    wide = jax.ShapeDtypeStruct((clusters + 1, QUAD * CL, CL), f32)
    acc = jax.ShapeDtypeStruct((clusters + 1, CL, CL), f32)
    return pl.pallas_call(
        functools.partial(pair_kernel, here, clusters),
        out_shape=[left, wide, acc] if here else [result, acc],
        in_specs=[whole] * (len(tables) + (0 if here else 3)),
        out_specs=[whole] * (3 if here else 2),
        input_output_aliases={} if here else {len(tables) + 2: 1},
        scratch_shapes=[
            pltpu.VMEM((8, CL), jnp.int32),
            pltpu.SMEM((8, CL), jnp.int32),
            pltpu.SemaphoreType.DMA,
            pltpu.SMEM((8 * CL + UNROLL,), jnp.int32),
            pltpu.VMEM((places, DEPTH, QUAD * CL), bf16),
            pltpu.VMEM((places, 16, CL), f32),
        ],
        compiler_params=pltpu.CompilerParams(vmem_limit_bytes=32 * 1024 * 1024),
        cost_estimate=pl.CostEstimate(
            flops=2_000_000_000, bytes_accessed=(40 if here else 80) * 1024 * 1024, transcendentals=10_000_000
        ),
        name="pairs_here" if here else "pairs_across",
    )(*tables, *(kept or ()))


def pack_kernel(*refs):
    sent, out = refs[5:7]
    points, weights, density, near_pairs, gap_pairs = refs[7:12]
    copies = [pltpu.make_async_copy(refs[k], refs[7 + k], refs[12].at[k]) for k in range(5)]
    for copy in copies:
        copy.start()
    for copy in copies:
        copy.wait()
    for q in range(QUAD):
        for c in range(3):
            out[4 * q + c : 4 * q + c + 1, :] = points[c, q : q + 1, :]
        out[4 * q + 3 : 4 * q + 4, :] = weights[q : q + 1, :]
    out[12:14, :] = density[...]
    out[14:16, :] = jnp.zeros((2, out.shape[1]), f32)
    for k in range(3):
        out[14:15, k * CL : k * CL + near_pairs.shape[1]] = near_pairs[k : k + 1, :].astype(f32)
        out[15:16, k * CL : k * CL + gap_pairs.shape[1]] = gap_pairs[k : k + 1, :].astype(f32)
    sent[...] = out[...]


def packed(points, weights, density, near_pairs, gap_pairs):
    whole = pl.BlockSpec(memory_space=pltpu.VMEM)
    return pl.pallas_call(
        pack_kernel,
        out_shape=[jax.ShapeDtypeStruct((16, points.shape[2]), f32)] * 2,
        in_specs=[pl.BlockSpec(memory_space=pltpu.HBM)] * 5,
        out_specs=[whole] * 2,
        scratch_shapes=[pltpu.VMEM(x.shape, x.dtype) for x in (points, weights, density, near_pairs, gap_pairs)]
        + [pltpu.SemaphoreType.DMA((5,))],
        compiler_params=pltpu.CompilerParams(vmem_limit_bytes=8 * 1024 * 1024),
        name="pack",
    )(*[pltpu.with_memory_space_constraint(x, pltpu.HBM) for x in (points, weights, density, near_pairs, gap_pairs)])


near_partners = (
    lambda i: i ^ 1,
    lambda i: ((i + 1) ^ 1) - 1,
    lambda i: i ^ 2,
    lambda i: ((i + 2) ^ 2) - 2,
)


def swapped(block, axis, partner):
    size = lax.axis_size(axis)
    route = [(i, partner(i)) for i in range(size) if 0 <= partner(i) < size]
    return lax.ppermute(block, axis, route)


def per_device(points, weights, density, near_pairs, gap_pairs):
    sent, local = packed(points, weights, density, near_pairs, gap_pairs)
    tables = [local]
    for slot in TABLE_ORDER:
        if slot > 4:
            tables.append(swapped(sent, "section", lambda i, k=slot - 4: i ^ k))
        else:
            tables.append(swapped(sent, "dev", near_partners[slot - 1]))
    kept = pair_sums(tables[:1])
    return pair_sums(tables, kept)[0]


def solution(mesh):
    placed = (
        P(None, None, ("section", "dev")),
        P(None, ("section", "dev")),
        P(None, ("section", "dev")),
        P(None, ("section", "dev")),
        P(None, ("section", "dev")),
    )
    return jax.shard_map(
        per_device,
        mesh=mesh,
        in_specs=placed,
        out_specs=P(None, ("section", "dev")),
        check_vma=False,
    )
```

```python
import functools
import math

import jax
import jax.numpy as jnp
from jax import lax
from jax.experimental import pallas as pl
from jax.experimental.pallas import tpu as pltpu
from jax.sharding import PartitionSpec as P

CL = 128
QUAD = 3
DEPTH = 48
TURNED = 64
UNROLL = 14
TABLE_ORDER = (3, 7, 4, 5, 6, 2, 1)

smoothing = 0.02
green_scale = 0.25 / math.pi
f32 = jnp.float32
bf16 = jnp.bfloat16


def rounded(x, magic):
    return (x + magic) - magic


def row_ids(like):
    return lax.broadcasted_iota(jnp.int32, like.shape, 0)


def parts_of(tile, row_limit):
    rows = row_ids(tile)
    live = jnp.logical_and(jnp.bitwise_and(rows, 3) < 3, rows < row_limit)
    x = jnp.where(live, tile, 0.0)
    high = rounded(x, 49152.0)
    rest = x - high
    mid = rounded(rest, 96.0)
    low = rounded(rest - mid, 0.1875)
    rest = mid + low
    sq_high = high * high
    sq_rest = rest * (high + high + rest)

    def row_sum(v):
        u = v + pltpu.roll(v, 7, 0)
        return u + pltpu.roll(u, 6, 0)

    return high, mid, low, row_sum(sq_high), row_sum(sq_rest)


def square_parts(sum_high, sum_rest):
    rows = row_ids(sum_high)
    upper = rows < 4
    v = jnp.where(upper, sum_high, sum_rest)
    one = rounded(v, jnp.where(upper, 196608.0, 768.0))
    rest = v - one
    two = rounded(rest, jnp.where(upper, 768.0, 3.0))
    three = rest - two
    place = jnp.bitwise_and(rows, 3)
    return jnp.where(place == 0, one, jnp.where(place == 1, two, jnp.where(place == 2, three, 0.0)))


def point_features(tile0, tile1):
    h0, m0, l0, sh0, sr0 = parts_of(tile0, 8)
    h1, m1, l1, sh1, sr1 = parts_of(tile1, 3)

    def spread(v, row):
        return jnp.broadcast_to(v[row : row + 1], v.shape)

    turn = lambda v: pltpu.roll(v, 4, 0)
    return (
        (h0, m0, l0, turn(l0), spread(sh0, 0), spread(sr0, 0)),
        (turn(h0), turn(m0), turn(l0), l0, spread(sh0, 4), spread(sr0, 4)),
        (h1, m1, l1, turn(l1), spread(sh1, 0), spread(sr1, 0)),
    )


def right_features(tile0, tile1):
    rows = row_ids(tile0)
    out = []
    for high, mid, low, low_turned, sum_high, sum_rest in point_features(tile0, tile1):
        ones = jnp.where(rows < 6, 1.0, 0.0)
        g0 = jnp.where(rows < 3, high, jnp.where(rows < 6, ones, pltpu.roll(mid, 6, 0)))
        g1 = square_parts(sum_high, sum_rest + smoothing * smoothing)
        g1 = jnp.where(rows == 7, pltpu.roll(mid, 5, 0), g1)
        g4 = jnp.where(rows < 4, mid, low_turned)
        out.append(jnp.concatenate([g0, g1, g0, g0, g4, g4], 0).astype(bf16))
    return out


def left_features(tile0, tile1):
    rows = row_ids(tile0)
    out = []
    for high, mid, low, low_turned, sum_high, sum_rest in point_features(tile0, tile1):
        sq = square_parts(sum_high, sum_rest)
        sq_high = pltpu.roll(sq, 3, 0)
        sq_rest = pltpu.roll(sq, 7, 0)
        first = rows < 3
        mids = jnp.logical_and(rows >= 3, rows < 6)
        h2 = jnp.where(first, -2.0 * high, 0.0)
        m2 = jnp.where(first, -2.0 * mid, 0.0)
        l2 = jnp.where(first, -2.0 * low, 0.0)
        b0 = jnp.where(mids, sq_high, h2)
        b1 = jnp.where(jnp.bitwise_and(rows, 3) < 3, 1.0, jnp.where(rows == 7, pltpu.roll(l2, 5, 0), 0.0))
        b3 = jnp.where(rows < 6, l2, pltpu.roll(l2, 6, 0))
        b2 = jnp.where(mids, sq_rest, m2)
        b4 = h2 + pltpu.roll(h2, 4, 0)
        b5 = m2 + pltpu.roll(m2, 4, 0)
        out.append(jnp.concatenate([b0, b1, b2, b3, b4, b5], 0))
    return out


def pair_codes(here, local, others, codes):
    def lists(table, row):
        return [table[row : row + 1, k * CL : (k + 1) * CL].astype(jnp.int32) for k in range(3)]

    low5 = lambda v: jnp.bitwise_and(v, 31)
    up5 = lambda v: lax.shift_right_logical(v, 5)

    def coded(valid, here, slot, there):
        return jnp.where(valid, low5(here) + (slot * 32 + low5(there)) * 256, -1)

    first, second, listed = lists(local, 14)
    me = jnp.broadcast_to(up5(first[:, 0:1]), first.shape)
    my_dev, dev = low5(me), low5(up5(second))
    slot = jnp.full(first.shape, 4, jnp.int32)
    slot = jnp.where(dev == jnp.bitwise_xor(my_dev, 2), 3, slot)
    slot = jnp.where(dev == jnp.bitwise_xor(my_dev + 1, 1) - 1, 2, slot)
    slot = jnp.where(dev == jnp.bitwise_xor(my_dev, 1), 1, slot)
    slot = jnp.where(dev == my_dev, 0, slot)
    inside = slot == 0
    if here:
        codes[0:1, :] = coded(jnp.logical_and(listed > 0, inside), first, 0, second)
        inside = jnp.logical_and(inside, first != second)
        codes[1:2, :] = coded(jnp.logical_and(listed > 0, inside), second, 0, first)
        return
    codes[0:1, :] = coded(jnp.logical_and(listed > 0, slot > 0), first, slot, second)
    for slot_in in range(1, 5):
        first, second, listed = lists(others[slot_in - 1], 14)
        valid = jnp.logical_and(listed > 0, up5(second) == me)
        codes[slot_in : slot_in + 1, :] = coded(valid, second, slot_in, first)
    first, second, listed = lists(local, 15)
    slot = 4 + jnp.bitwise_xor(up5(me), up5(up5(second)))
    row = coded(listed > 0, first, slot, second)
    lanes = lax.broadcasted_iota(jnp.int32, row.shape, 1)
    for slot_in in range(5, 8):
        first, second, listed = lists(others[slot_in - 1], 15)
        valid = jnp.logical_and(listed > 0, up5(second) == me)
        incoming = coded(valid, second, slot_in, first)
        row = jnp.where(lanes < 32 * (slot_in - 4), row, pltpu.roll(incoming, 32 * (slot_in - 4), 1))
    codes[5:6, :] = row


WIDE = 8


def pair_kernel(here, clusters, *refs):
    tables = refs[:1] if here else refs[:8]
    local = tables[0]
    refs = refs[len(tables) :]
    if not here:
        tables = [local] + [tables[1 + TABLE_ORDER.index(slot)] for slot in range(1, 8)]
    if here:
        left, wide_w, acc = refs[:3]
        refs = refs[3:]
    else:
        left, wide_w, _, out, acc = refs[:5]
        refs = refs[5:]
    codes, codes_smem, sem, todo, right, raw = refs
    used = tables if here else tables[1:]
    base = 0 if here else clusters

    pair_codes(here, local, tables[1:], codes)
    lists_copy = pltpu.make_async_copy(codes, codes_smem, sem)
    lists_copy.start()

    def prepare_left(n, carry):
        for u in range(WIDE):
            c = n * WIDE + u
            lanes = pl.ds(pl.multiple_of(c * CL, CL), CL)
            tile0, tile1 = local[0:8, lanes], local[8:16, lanes]
            weight_rows = (tile0[3:4], tile0[7:8], tile1[3:4])
            for q, block in enumerate(left_features(tile0, tile1)):
                weight = jnp.broadcast_to(weight_rows[q] * green_scale, (8, CL))
                block = jnp.concatenate([block, weight, jnp.zeros((TURNED - DEPTH - 8, CL), f32)], 0)
                turned = jnp.transpose(block)
                left[c, q * CL : (q + 1) * CL, 0:TURNED] = turned.astype(bf16)
                wide_w[c, q * CL : (q + 1) * CL, :] = jnp.broadcast_to(turned[:, DEPTH : DEPTH + 1], (CL, CL))
            acc[c] = jnp.zeros((CL, CL), f32)
        return carry

    if here:
        lax.fori_loop(0, clusters // WIDE, prepare_left, 0)
    lists_copy.wait()

    steps = clusters // WIDE
    rows_of_codes = 2 if here else 6
    count = 0
    for table in range(len(used)):

        def prepare_right(n, count):
            lanes = pl.ds(pl.multiple_of(n * (WIDE * CL), WIDE * CL), WIDE * CL)
            tile0, tile1 = used[table][0:8, lanes], used[table][8:16, lanes]
            blocks = right_features(tile0, tile1)
            for u in range(WIDE):
                place = table * clusters + n * WIDE + u
                cut = slice(u * CL, (u + 1) * CL)
                for q in range(QUAD):
                    right[place, :, q * CL : (q + 1) * CL] = blocks[q][:, cut]
                raw[place, 0:8, :] = tile0[:, cut]
                raw[place, 8:16, :] = tile1[:, cut]
            rows = range(2) if here else ([table] if table < 6 else [])
            for row in rows:
                for u in range(CL // steps):
                    code = codes_smem[row, n * (CL // steps) + u]
                    todo[count] = code
                    count = count + (code >= 0).astype(jnp.int32)
            return count

        count = lax.fori_loop(0, steps, prepare_right, count)
    for extra in range(UNROLL - 1):
        todo[count + extra] = clusters + base * 256

    def tile_of(i, j):
        weight_b = (raw[j, 3:4, :], raw[j, 7:8, :], raw[j, 11:12, :])
        far = right[j]
        total = None
        for p in range(QUAD):
            near = left[i, p * CL : (p + 1) * CL, 0:DEPTH]
            dist = jnp.dot(near, far, preferred_element_type=f32)
            row = None
            for q in range(QUAD):
                term = weight_b[q] * lax.rsqrt(dist[:, q * CL : (q + 1) * CL])
                row = term if row is None else row + term
            row = row * wide_w[i, p * CL : (p + 1) * CL, :]
            total = row if total is None else total + row
        return total

    lower = lax.broadcasted_iota(jnp.int32, (1, CL), 1) < CL // 2

    def group(g, carry):
        done = []
        for u in range(UNROLL):
            code = todo[g * UNROLL + u]
            i = jnp.bitwise_and(code, 255)
            j = lax.shift_right_logical(code, 8) - base
            done.append((i, j, tile_of(i, j)))
        for i, j, tile in done:
            dens0, dens1 = raw[j, 12:13, :], raw[j, 13:14, :]
            same = tile * jnp.where(lower, dens0, dens1)
            other = tile * jnp.where(lower, dens1, dens0)
            acc[i] += same + pltpu.roll(other, CL // 2, 1)
        return carry

    lax.fori_loop(0, lax.div(count + UNROLL - 1, UNROLL), group, 0)

    if here:
        return

    rows = lax.broadcasted_iota(jnp.int32, (8, 2 * CL), 0)
    lanes_of = jnp.bitwise_and(lax.broadcasted_iota(jnp.int32, (8, 2 * CL), 1), CL - 1)
    chosen = jnp.where(rows == lanes_of // (CL // 2), 1.0, 0.0).astype(bf16)

    def finish(n, carry):
        for u in range(8):
            c = n * 8 + u
            lanes = pl.ds(pl.multiple_of(c * CL, CL), CL)
            value = acc[c]
            high = value.astype(bf16)
            low = (value - high.astype(f32)).astype(bf16)
            both = jnp.concatenate([high, low], 1)
            sums = lax.dot_general(chosen, both, (((1,), (1,)), ((), ())), preferred_element_type=f32)
            out[:, lanes] = sums[0:2]
        return carry

    lax.fori_loop(0, clusters // 8, finish, 0)


def pair_sums(tables, kept=None):
    here = kept is None
    panels = tables[0].shape[1]
    clusters = panels // CL
    places = (1 if here else len(tables) - 1) * clusters
    whole = pl.BlockSpec(memory_space=pltpu.VMEM)
    result = jax.ShapeDtypeStruct((2, panels), f32)
    left = jax.ShapeDtypeStruct((clusters + 1, QUAD * CL, CL), bf16)
    wide = jax.ShapeDtypeStruct((clusters + 1, QUAD * CL, CL), f32)
    acc = jax.ShapeDtypeStruct((clusters + 1, CL, CL), f32)
    return pl.pallas_call(
        functools.partial(pair_kernel, here, clusters),
        out_shape=[left, wide, acc] if here else [result, acc],
        in_specs=[whole] * (len(tables) + (0 if here else 3)),
        out_specs=[whole] * (3 if here else 2),
        input_output_aliases={} if here else {len(tables) + 2: 1},
        scratch_shapes=[
            pltpu.VMEM((8, CL), jnp.int32),
            pltpu.SMEM((8, CL), jnp.int32),
            pltpu.SemaphoreType.DMA,
            pltpu.SMEM((8 * CL + UNROLL,), jnp.int32),
            pltpu.VMEM((places, DEPTH, QUAD * CL), bf16),
            pltpu.VMEM((places, 16, CL), f32),
        ],
        compiler_params=pltpu.CompilerParams(vmem_limit_bytes=32 * 1024 * 1024),
        cost_estimate=pl.CostEstimate(
            flops=2_000_000_000, bytes_accessed=(40 if here else 80) * 1024 * 1024, transcendentals=10_000_000
        ),
        name="pairs_here" if here else "pairs_across",
    )(*tables, *(kept or ()))


def pack_kernel(*refs):
    out = refs[5]
    points, weights, density, near_pairs, gap_pairs = refs[6:11]
    copies = [pltpu.make_async_copy(refs[k], refs[6 + k], refs[11].at[k]) for k in range(5)]
    for copy in copies:
        copy.start()
    for copy in copies:
        copy.wait()
    for q in range(QUAD):
        for c in range(3):
            out[4 * q + c : 4 * q + c + 1, :] = points[c, q : q + 1, :]
        out[4 * q + 3 : 4 * q + 4, :] = weights[q : q + 1, :]
    out[12:14, :] = density[...]
    out[14:16, :] = jnp.zeros((2, out.shape[1]), f32)
    for k in range(3):
        out[14:15, k * CL : k * CL + near_pairs.shape[1]] = near_pairs[k : k + 1, :].astype(f32)
        out[15:16, k * CL : k * CL + gap_pairs.shape[1]] = gap_pairs[k : k + 1, :].astype(f32)


def packed(points, weights, density, near_pairs, gap_pairs):
    whole = pl.BlockSpec(memory_space=pltpu.VMEM)
    return pl.pallas_call(
        pack_kernel,
        out_shape=jax.ShapeDtypeStruct((16, points.shape[2]), f32),
        in_specs=[pl.BlockSpec(memory_space=pltpu.HBM)] * 5,
        out_specs=whole,
        scratch_shapes=[pltpu.VMEM(x.shape, x.dtype) for x in (points, weights, density, near_pairs, gap_pairs)]
        + [pltpu.SemaphoreType.DMA((5,))],
        compiler_params=pltpu.CompilerParams(vmem_limit_bytes=8 * 1024 * 1024),
        name="pack",
    )(*[pltpu.with_memory_space_constraint(x, pltpu.HBM) for x in (points, weights, density, near_pairs, gap_pairs)])


near_partners = (
    lambda i: i ^ 1,
    lambda i: ((i + 1) ^ 1) - 1,
    lambda i: i ^ 2,
    lambda i: ((i + 2) ^ 2) - 2,
)


def swapped(block, axis, partner):
    size = lax.axis_size(axis)
    route = [(i, partner(i)) for i in range(size) if 0 <= partner(i) < size]
    return lax.ppermute(block, axis, route)


def per_device(points, weights, density, near_pairs, gap_pairs):
    local = packed(points, weights, density, near_pairs, gap_pairs)
    tables = [local]
    for slot in TABLE_ORDER:
        if slot > 4:
            tables.append(swapped(local, "section", lambda i, k=slot - 4: i ^ k))
        else:
            tables.append(swapped(local, "dev", near_partners[slot - 1]))
    kept = pair_sums(tables[:1])
    return pair_sums(tables, kept)[0]


def solution(mesh):
    placed = (
        P(None, None, ("section", "dev")),
        P(None, ("section", "dev")),
        P(None, ("section", "dev")),
        P(None, ("section", "dev")),
        P(None, ("section", "dev")),
    )
    return jax.shard_map(
        per_device,
        mesh=mesh,
        in_specs=placed,
        out_specs=P(None, ("section", "dev")),
        check_vma=False,
    )
```

```python
import functools
import math

import jax
import jax.numpy as jnp
from jax import lax
from jax.experimental import pallas as pl
from jax.experimental.pallas import tpu as pltpu
from jax.sharding import PartitionSpec as P

CL = 128
QUAD = 3
DEPTH = 48
TURNED = 64
UNROLL = 14
TABLE_ORDER = (3, 7, 4, 5, 6, 2, 1)

smoothing = 0.02
green_scale = 0.25 / math.pi
f32 = jnp.float32
bf16 = jnp.bfloat16


def rounded(x, magic):
    return (x + magic) - magic


def row_ids(like):
    return lax.broadcasted_iota(jnp.int32, like.shape, 0)


def parts_of(tile, row_limit):
    rows = row_ids(tile)
    live = jnp.logical_and(jnp.bitwise_and(rows, 3) < 3, rows < row_limit)
    x = jnp.where(live, tile, 0.0)
    high = rounded(x, 49152.0)
    rest = x - high
    mid = rounded(rest, 96.0)
    low = rounded(rest - mid, 0.1875)
    rest = mid + low
    sq_high = high * high
    sq_rest = rest * (high + high + rest)

    def row_sum(v):
        u = v + pltpu.roll(v, 7, 0)
        return u + pltpu.roll(u, 6, 0)

    return high, mid, low, row_sum(sq_high), row_sum(sq_rest)


def square_parts(sum_high, sum_rest):
    rows = row_ids(sum_high)
    upper = rows < 4
    v = jnp.where(upper, sum_high, sum_rest)
    one = rounded(v, jnp.where(upper, 196608.0, 768.0))
    rest = v - one
    two = rounded(rest, jnp.where(upper, 768.0, 3.0))
    three = rest - two
    place = jnp.bitwise_and(rows, 3)
    return jnp.where(place == 0, one, jnp.where(place == 1, two, jnp.where(place == 2, three, 0.0)))


def point_features(tile0, tile1):
    h0, m0, l0, sh0, sr0 = parts_of(tile0, 8)
    h1, m1, l1, sh1, sr1 = parts_of(tile1, 3)

    def spread(v, row):
        return jnp.broadcast_to(v[row : row + 1], v.shape)

    turn = lambda v: pltpu.roll(v, 4, 0)
    return (
        (h0, m0, l0, turn(l0), spread(sh0, 0), spread(sr0, 0)),
        (turn(h0), turn(m0), turn(l0), l0, spread(sh0, 4), spread(sr0, 4)),
        (h1, m1, l1, turn(l1), spread(sh1, 0), spread(sr1, 0)),
    )


def right_features(tile0, tile1):
    rows = row_ids(tile0)
    out = []
    for high, mid, low, low_turned, sum_high, sum_rest in point_features(tile0, tile1):
        ones = jnp.where(rows < 6, 1.0, 0.0)
        g0 = jnp.where(rows < 3, high, jnp.where(rows < 6, ones, pltpu.roll(mid, 6, 0)))
        g1 = square_parts(sum_high, sum_rest + smoothing * smoothing)
        g1 = jnp.where(rows == 7, pltpu.roll(mid, 5, 0), g1)
        g4 = jnp.where(rows < 4, mid, low_turned)
        out.append(jnp.concatenate([g0, g1, g0, g0, g4, g4], 0).astype(bf16))
    return out


def left_features(tile0, tile1):
    rows = row_ids(tile0)
    out = []
    for high, mid, low, low_turned, sum_high, sum_rest in point_features(tile0, tile1):
        sq = square_parts(sum_high, sum_rest)
        sq_high = pltpu.roll(sq, 3, 0)
        sq_rest = pltpu.roll(sq, 7, 0)
        first = rows < 3
        mids = jnp.logical_and(rows >= 3, rows < 6)
        h2 = jnp.where(first, -2.0 * high, 0.0)
        m2 = jnp.where(first, -2.0 * mid, 0.0)
        l2 = jnp.where(first, -2.0 * low, 0.0)
        b0 = jnp.where(mids, sq_high, h2)
        b1 = jnp.where(jnp.bitwise_and(rows, 3) < 3, 1.0, jnp.where(rows == 7, pltpu.roll(l2, 5, 0), 0.0))
        b3 = jnp.where(rows < 6, l2, pltpu.roll(l2, 6, 0))
        b2 = jnp.where(mids, sq_rest, m2)
        b4 = h2 + pltpu.roll(h2, 4, 0)
        b5 = m2 + pltpu.roll(m2, 4, 0)
        out.append(jnp.concatenate([b0, b1, b2, b3, b4, b5], 0))
    return out


def pair_codes(here, local, others, codes):
    def lists(table, row):
        return [table[row : row + 1, k * CL : (k + 1) * CL].astype(jnp.int32) for k in range(3)]

    low5 = lambda v: jnp.bitwise_and(v, 31)
    up5 = lambda v: lax.shift_right_logical(v, 5)

    def coded(valid, here, slot, there):
        return jnp.where(valid, low5(here) + (slot * 32 + low5(there)) * 256, -1)

    first, second, listed = lists(local, 14)
    me = jnp.broadcast_to(up5(first[:, 0:1]), first.shape)
    my_dev, dev = low5(me), low5(up5(second))
    slot = jnp.full(first.shape, 4, jnp.int32)
    slot = jnp.where(dev == jnp.bitwise_xor(my_dev, 2), 3, slot)
    slot = jnp.where(dev == jnp.bitwise_xor(my_dev + 1, 1) - 1, 2, slot)
    slot = jnp.where(dev == jnp.bitwise_xor(my_dev, 1), 1, slot)
    slot = jnp.where(dev == my_dev, 0, slot)
    inside = slot == 0
    if here:
        codes[0:1, :] = coded(jnp.logical_and(listed > 0, inside), first, 0, second)
        inside = jnp.logical_and(inside, first != second)
        codes[1:2, :] = coded(jnp.logical_and(listed > 0, inside), second, 0, first)
        return
    codes[0:1, :] = coded(jnp.logical_and(listed > 0, slot > 0), first, slot, second)
    for slot_in in range(1, 5):
        first, second, listed = lists(others[slot_in - 1], 14)
        valid = jnp.logical_and(listed > 0, up5(second) == me)
        codes[slot_in : slot_in + 1, :] = coded(valid, second, slot_in, first)
    first, second, listed = lists(local, 15)
    slot = 4 + jnp.bitwise_xor(up5(me), up5(up5(second)))
    row = coded(listed > 0, first, slot, second)
    lanes = lax.broadcasted_iota(jnp.int32, row.shape, 1)
    for slot_in in range(5, 8):
        first, second, listed = lists(others[slot_in - 1], 15)
        valid = jnp.logical_and(listed > 0, up5(second) == me)
        incoming = coded(valid, second, slot_in, first)
        row = jnp.where(lanes < 32 * (slot_in - 4), row, pltpu.roll(incoming, 32 * (slot_in - 4), 1))
    codes[5:6, :] = row


WIDE = 8


def pair_kernel(here, clusters, *refs):
    tables = refs[:1] if here else refs[:8]
    local = tables[0]
    refs = refs[len(tables) :]
    if not here:
        tables = [local] + [tables[1 + TABLE_ORDER.index(slot)] for slot in range(1, 8)]
    if here:
        left, wide_w, acc = refs[:3]
        refs = refs[3:]
    else:
        left, wide_w, _, out, acc = refs[:5]
        refs = refs[5:]
    codes, codes_smem, sem, todo, right, raw = refs
    used = tables if here else tables[1:]
    base = 0 if here else clusters

    pair_codes(here, local, tables[1:], codes)
    lists_copy = pltpu.make_async_copy(codes, codes_smem, sem)
    lists_copy.start()

    def prepare_left(n, carry):
        for u in range(WIDE):
            c = n * WIDE + u
            lanes = pl.ds(pl.multiple_of(c * CL, CL), CL)
            tile0, tile1 = local[0:8, lanes], local[8:16, lanes]
            weight_rows = (tile0[3:4], tile0[7:8], tile1[3:4])
            for q, block in enumerate(left_features(tile0, tile1)):
                weight = jnp.broadcast_to(weight_rows[q] * green_scale, (8, CL))
                block = jnp.concatenate([block, weight, jnp.zeros((TURNED - DEPTH - 8, CL), f32)], 0)
                turned = jnp.transpose(block)
                left[c, q * CL : (q + 1) * CL, 0:TURNED] = turned.astype(bf16)
                wide_w[c, q * CL : (q + 1) * CL, :] = jnp.broadcast_to(turned[:, DEPTH : DEPTH + 1], (CL, CL))
            acc[c] = jnp.zeros((CL, CL), f32)
        return carry

    if here:
        lax.fori_loop(0, clusters // WIDE, prepare_left, 0)
    lists_copy.wait()

    steps = clusters // WIDE
    rows_of_codes = 2 if here else 6
    count = 0
    for table in range(len(used)):

        def prepare_right(n, count):
            lanes = pl.ds(pl.multiple_of(n * (WIDE * CL), WIDE * CL), WIDE * CL)
            tile0, tile1 = used[table][0:8, lanes], used[table][8:16, lanes]
            blocks = right_features(tile0, tile1)
            for u in range(WIDE):
                place = table * clusters + n * WIDE + u
                cut = slice(u * CL, (u + 1) * CL)
                for q in range(QUAD):
                    right[place, :, q * CL : (q + 1) * CL] = blocks[q][:, cut]
                raw[place, 0:8, :] = tile0[:, cut]
                raw[place, 8:16, :] = tile1[:, cut]
            rows = range(2) if here else ([table] if table < 6 else [])
            for row in rows:
                for u in range(CL // steps):
                    code = codes_smem[row, n * (CL // steps) + u]
                    todo[count] = code
                    count = count + (code >= 0).astype(jnp.int32)
            return count

        count = lax.fori_loop(0, steps, prepare_right, count)
    for extra in range(UNROLL - 1):
        todo[count + extra] = clusters + base * 256

    def tile_of(i, j):
        weight_b = (raw[j, 3:4, :], raw[j, 7:8, :], raw[j, 11:12, :])
        far = right[j]
        total = None
        for p in range(QUAD):
            near = left[i, p * CL : (p + 1) * CL, 0:DEPTH]
            dist = jnp.dot(near, far, preferred_element_type=f32)
            row = None
            for q in range(QUAD):
                term = weight_b[q] * lax.rsqrt(dist[:, q * CL : (q + 1) * CL])
                row = term if row is None else row + term
            row = row * wide_w[i, p * CL : (p + 1) * CL, :]
            total = row if total is None else total + row
        return total

    lower = lax.broadcasted_iota(jnp.int32, (1, CL), 1) < CL // 2

    def group(g, carry):
        done = []
        for u in range(UNROLL):
            code = todo[g * UNROLL + u]
            i = jnp.bitwise_and(code, 255)
            j = lax.shift_right_logical(code, 8) - base
            done.append((i, j, tile_of(i, j)))
        for i, j, tile in done:
            dens0, dens1 = raw[j, 12:13, :], raw[j, 13:14, :]
            same = tile * jnp.where(lower, dens0, dens1)
            other = tile * jnp.where(lower, dens1, dens0)
            acc[i] += same + pltpu.roll(other, CL // 2, 1)
        return carry

    lax.fori_loop(0, lax.div(count + UNROLL - 1, UNROLL), group, 0)

    if here:
        return

    rows = lax.broadcasted_iota(jnp.int32, (8, 2 * CL), 0)
    lanes_of = jnp.bitwise_and(lax.broadcasted_iota(jnp.int32, (8, 2 * CL), 1), CL - 1)
    chosen = jnp.where(rows == lanes_of // (CL // 2), 1.0, 0.0).astype(bf16)

    def finish(n, carry):
        for u in range(16):
            c = n * 16 + u
            lanes = pl.ds(pl.multiple_of(c * CL, CL), CL)
            value = acc[c]
            high = value.astype(bf16)
            low = (value - high.astype(f32)).astype(bf16)
            both = jnp.concatenate([high, low], 1)
            sums = lax.dot_general(chosen, both, (((1,), (1,)), ((), ())), preferred_element_type=f32)
            out[:, lanes] = sums[0:2]
        return carry

    lax.fori_loop(0, clusters // 16, finish, 0)


def pair_sums(tables, kept=None):
    here = kept is None
    panels = tables[0].shape[1]
    clusters = panels // CL
    places = (1 if here else len(tables) - 1) * clusters
    whole = pl.BlockSpec(memory_space=pltpu.VMEM)
    result = jax.ShapeDtypeStruct((2, panels), f32)
    left = jax.ShapeDtypeStruct((clusters + 1, QUAD * CL, CL), bf16)
    wide = jax.ShapeDtypeStruct((clusters + 1, QUAD * CL, CL), f32)
    acc = jax.ShapeDtypeStruct((clusters + 1, CL, CL), f32)
    return pl.pallas_call(
        functools.partial(pair_kernel, here, clusters),
        out_shape=[left, wide, acc] if here else [result, acc],
        in_specs=[whole] * (len(tables) + (0 if here else 3)),
        out_specs=[whole] * (3 if here else 2),
        input_output_aliases={} if here else {len(tables) + 2: 1},
        scratch_shapes=[
            pltpu.VMEM((8, CL), jnp.int32),
            pltpu.SMEM((8, CL), jnp.int32),
            pltpu.SemaphoreType.DMA,
            pltpu.SMEM((8 * CL + UNROLL,), jnp.int32),
            pltpu.VMEM((places, DEPTH, QUAD * CL), bf16),
            pltpu.VMEM((places, 16, CL), f32),
        ],
        compiler_params=pltpu.CompilerParams(vmem_limit_bytes=32 * 1024 * 1024),
        cost_estimate=pl.CostEstimate(
            flops=2_000_000_000, bytes_accessed=(40 if here else 80) * 1024 * 1024, transcendentals=10_000_000
        ),
        name="pairs_here" if here else "pairs_across",
    )(*tables, *(kept or ()))


def pack_kernel(*refs):
    out = refs[5]
    points, weights, density, near_pairs, gap_pairs = refs[6:11]
    copies = [pltpu.make_async_copy(refs[k], refs[6 + k], refs[11].at[k]) for k in range(5)]
    for copy in copies:
        copy.start()
    for copy in copies:
        copy.wait()
    for q in range(QUAD):
        for c in range(3):
            out[4 * q + c : 4 * q + c + 1, :] = points[c, q : q + 1, :]
        out[4 * q + 3 : 4 * q + 4, :] = weights[q : q + 1, :]
    out[12:14, :] = density[...]
    out[14:16, :] = jnp.zeros((2, out.shape[1]), f32)
    for k in range(3):
        out[14:15, k * CL : k * CL + near_pairs.shape[1]] = near_pairs[k : k + 1, :].astype(f32)
        out[15:16, k * CL : k * CL + gap_pairs.shape[1]] = gap_pairs[k : k + 1, :].astype(f32)


def packed(points, weights, density, near_pairs, gap_pairs):
    whole = pl.BlockSpec(memory_space=pltpu.VMEM)
    return pl.pallas_call(
        pack_kernel,
        out_shape=jax.ShapeDtypeStruct((16, points.shape[2]), f32),
        in_specs=[pl.BlockSpec(memory_space=pltpu.HBM)] * 5,
        out_specs=whole,
        scratch_shapes=[pltpu.VMEM(x.shape, x.dtype) for x in (points, weights, density, near_pairs, gap_pairs)]
        + [pltpu.SemaphoreType.DMA((5,))],
        compiler_params=pltpu.CompilerParams(vmem_limit_bytes=8 * 1024 * 1024),
        name="pack",
    )(*[pltpu.with_memory_space_constraint(x, pltpu.HBM) for x in (points, weights, density, near_pairs, gap_pairs)])


near_partners = (
    lambda i: i ^ 1,
    lambda i: ((i + 1) ^ 1) - 1,
    lambda i: i ^ 2,
    lambda i: ((i + 2) ^ 2) - 2,
)


def swapped(block, axis, partner):
    size = lax.axis_size(axis)
    route = [(i, partner(i)) for i in range(size) if 0 <= partner(i) < size]
    return lax.ppermute(block, axis, route)


def per_device(points, weights, density, near_pairs, gap_pairs):
    local = packed(points, weights, density, near_pairs, gap_pairs)
    tables = [local]
    for slot in TABLE_ORDER:
        if slot > 4:
            tables.append(swapped(local, "section", lambda i, k=slot - 4: i ^ k))
        else:
            tables.append(swapped(local, "dev", near_partners[slot - 1]))
    kept = pair_sums(tables[:1])
    return pair_sums(tables, kept)[0]


def solution(mesh):
    placed = (
        P(None, None, ("section", "dev")),
        P(None, ("section", "dev")),
        P(None, ("section", "dev")),
        P(None, ("section", "dev")),
        P(None, ("section", "dev")),
    )
    return jax.shard_map(
        per_device,
        mesh=mesh,
        in_specs=placed,
        out_specs=P(None, ("section", "dev")),
        check_vma=False,
    )
```
